256 devices in a mesh: ctx: 64 (over y, z, x_lo), head: 4 (over x_hi, core).
Axes of the slice: x: 4 (x_hi: 2, x_lo: 2; x = x_hi * 2 + x_lo), y: 4, z: 8, core: 2. Of those that a mesh axis runs over, the one named last changes fastest.
Arguments:
- queries: bfloat16 [16384, 1024], P(('ctx', 'head')), may hold values from -7 to 7
- key_vecs: bfloat16 [16384, 128], P(('ctx', 'head')), may hold values from -7 to 7
- value_vecs: bfloat16 [16384, 128], P(('ctx', 'head')), may hold values from -6 to 6
- out_grad: bfloat16 [16384, 1024], P(('ctx', 'head')), may hold values from -192 to 192
Outputs:
- query_grad: bfloat16 [16384, 1024], P(('ctx', 'head'))
- key_grad: bfloat16 [16384, 128], P(('ctx', 'head'))
- value_grad: bfloat16 [16384, 128], P(('ctx', 'head'))
The draws below stay inside these ranges and needn't reach their ends.
All inputs are finite; a program needn't handle non-finite values.
Results may differ from the reference program's by a relative error of at most 0.035.
Values may be sent and summed in bfloat16 or wider, within the bound.
A program may use at most 128 MiB of HBM per device.

```python
import math
import jax
import jax.numpy as jnp
from jax import lax

QHEADS = 8
HEAD_DIM = 128
SEQ = 16384


def draw_queries(key, part):
    seeded = jax.random.fold_in(key, 11)
    row_width = QHEADS * HEAD_DIM
    drawn = jnp.clip(jax.random.normal(seeded, (SEQ, row_width), jnp.float32), -4.0, 4.0)
    return drawn.astype(jnp.bfloat16)


def draw_key_vecs(key, part):
    seeded = jax.random.fold_in(key, 12)
    drawn = jnp.clip(jax.random.normal(seeded, (SEQ, HEAD_DIM), jnp.float32), -4.0, 4.0)
    return drawn.astype(jnp.bfloat16)


def steps_of(stream_key, dims, pieces, smallest, largest):
    factor_of, own = 1.0, jax.random.fold_in(stream_key, 6)
    for dim, blocks in pieces:
        heights = jnp.exp(jax.random.uniform(jax.random.fold_in(own, dim), (blocks,), jnp.float32, smallest / len(pieces), largest / len(pieces)))
        factor_of = factor_of * jnp.repeat(heights, dims[dim] // blocks).reshape([-1 if axis == dim else 1 for axis in range(len(dims))])
    return factor_of


def bell_draw(key, extent, spread, limit, shards=(), held_as=jnp.bfloat16):
    level = steps_of(key, extent, shards, -0.22, 0.18) if shards else 1.0
    values = jax.random.normal(key, extent, jnp.float32) * spread * level
    return jnp.minimum(jnp.maximum(values, -limit), limit).astype(held_as)


def setup_inputs(seed: int = 0) -> dict:
    splits = jax.random.split(jax.random.key(seed), 5)
    return {
        "queries": draw_queries(jax.random.fold_in(splits[4], 71), 0),
        "key_vecs": draw_key_vecs(jax.random.fold_in(splits[4], 71), 0),
        "value_vecs": bell_draw(splits[2], (SEQ, HEAD_DIM), 1.0, 6.0, ((0, 256),)),
        "out_grad": bell_draw(splits[3], (SEQ, QHEADS * HEAD_DIM), (SEQ ** 0.5 / 4), 192.0, ((0, 256),)),
    }


def reference(queries, key_vecs, value_vecs, out_grad):
    seq_len = queries.shape[0]
    head_size = key_vecs.shape[1]
    head_count = queries.shape[1] // head_size
    scaling = head_size ** -0.5
    query_block = math.gcd(seq_len, 256)
    block_count = seq_len // query_block
    keys_wide = key_vecs.astype(jnp.float32)
    values_wide = value_vecs.astype(jnp.float32)
    query_blocks = queries.reshape(block_count, query_block, head_count, head_size)
    grad_blocks = out_grad.reshape(block_count, query_block, head_count, head_size)

    def advance(running, sliced):
        key_sum, value_sum = running
        query_part = sliced[0].astype(jnp.float32)
        grad_part = sliced[1].astype(jnp.float32)
        scores = jnp.einsum("qhd,kd->hqk", query_part, keys_wide) * scaling
        maxima = jnp.max(scores, axis=2, keepdims=True)
        weights = jnp.exp(scores - maxima)
        totals = jnp.sum(weights, axis=2, keepdims=True)
        weights_low = lax.optimization_barrier(weights.astype(jnp.bfloat16)).astype(jnp.float32)
        attended = (jnp.einsum("hqk,kd->hqd", weights_low, values_wide) / totals).astype(jnp.bfloat16)
        attended_wide = lax.optimization_barrier(attended).astype(jnp.float32)
        row_dots = jnp.einsum("qhd,hqd->hq", grad_part, attended_wide)
        log_totals = maxima + jnp.log(totals)
        chances = jnp.exp(scores - log_totals)
        chances_low = lax.optimization_barrier(chances.astype(jnp.bfloat16)).astype(jnp.float32)
        prob_grad = jnp.einsum("qhd,kd->hqk", grad_part, values_wide)
        score_grad = chances * (prob_grad - row_dots[:, :, None])
        score_grad = lax.optimization_barrier(score_grad.astype(jnp.bfloat16)).astype(jnp.float32)
        query_part_grad = scaling * jnp.einsum("hqk,kd->qhd", score_grad, keys_wide)
        key_sum = key_sum + scaling * jnp.einsum("hqk,qhd->kd", score_grad, query_part)
        value_sum = value_sum + jnp.einsum("hqk,qhd->kd", chances_low, grad_part)
        return (key_sum, value_sum), query_part_grad.astype(jnp.bfloat16).reshape(query_block, head_count * head_size)

    start_sums = (jnp.zeros((seq_len, head_size), jnp.float32), jnp.zeros((seq_len, head_size), jnp.float32))
    (key_sum, value_sum), query_grads = lax.scan(advance, start_sums, (query_blocks, grad_blocks))
    query_grad = query_grads.reshape(seq_len, head_count * head_size)
    return query_grad, key_sum.astype(jnp.bfloat16), value_sum.astype(jnp.bfloat16)
```

```python
import math

import jax
import jax.numpy as jnp
from jax import lax
from jax.experimental import pallas as pl
from jax.experimental.pallas import tpu as pltpu
from jax.sharding import PartitionSpec as P

F32, BF16 = jnp.float32, jnp.bfloat16
MESH = pl.DeviceIdType.MESH
NX, NY, NZ = 4, 4, 8
TOK = 64
DIM = 128
HALF = 512
RB = 512
KT = 1024
ROWS, KEYS = NX * RB, NY * KT
OFF = (0, 1, 3, 2)
SLOT = (0, 1, 3, 2)
SCALE = DIM**-0.5
LOG2_SCALE = SCALE * math.log2(math.e)
Z_ORDER = (1, 7, 2, 6, 3, 5, 4)


def nt(a, b):
    return lax.dot_general(a, b, (((1,), (1,)), ((), ())), preferred_element_type=F32)


def nn(a, b):
    return jnp.dot(a, b, preferred_element_type=F32)


def kernel(
    q_in, do_in, k_in, v_in, dq_out, dk_out, dv_out,
    qb, dob, kvb, kt, vt, w, mt, acc, st, sr, lse, rdn, fcol, dqt, dkv,
    sib_src, sib, r2_src, r2, y_src, yr, z_src, zr, dq_src, dqr,
    loc_sem, q_ss, q_rs, z_ss, z_rs, sb_ss, sb_rs, yk_ss, yk_rs, y2_ss, y2_rs,
    st_ss, st_rs, sib_ss, sib_rs, r2_ss, r2_rs, yr_ss, yr_rs, zr_ss, zr_rs, dq_ss, dq_rs,
):
    ctx, hd = lax.axis_index("ctx"), lax.axis_index("head")
    y, z = ctx // (2 * NZ), lax.rem(ctx // 2, NZ)
    x, c = (hd // 2) * 2 + lax.rem(ctx, 2), lax.rem(hd, 2)

    def dev(dx=0, dy=0, dz=0, dc=0):
        xx, yy = lax.rem(x + dx, NX), lax.rem(y + dy, NY)
        zz, cc = lax.rem(z + dz, NZ), lax.rem(c + dc, 2)
        return ((yy * NZ + zz) * 2 + lax.rem(xx, 2), (xx // 2) * 2 + cc)

    pending = []

    def send(src, dst, ss, rs, to):
        copy = pltpu.make_async_remote_copy(
            src_ref=src, dst_ref=dst, send_sem=ss, recv_sem=rs,
            device_id=to, device_id_type=MESH,
        )
        copy.start()
        pending.append(copy)

    def arrive(ref, rs):
        pltpu.make_async_remote_copy(
            src_ref=ref, dst_ref=ref, send_sem=rs, recv_sem=rs,
            device_id=dev(dc=1), device_id_type=MESH,
        ).wait_recv()

    def zrow(dz, core=0):
        zz = lax.rem(z + (NZ - dz), NZ)
        return pl.ds(pl.multiple_of(core * (NZ * TOK) + zz * TOK, TOK), TOK)

    def half(dc):
        return pl.ds(pl.multiple_of(lax.rem(c + dc, 2) * HALF, HALF), HALF)

    own = [
        pltpu.make_async_copy(k_in, kvb.at[0, zrow(0), 0:DIM], loc_sem.at[0]),
        pltpu.make_async_copy(v_in, kvb.at[0, zrow(0), DIM : 2 * DIM], loc_sem.at[1]),
        pltpu.make_async_copy(q_in.at[:, half(0)], qb.at[0, 0], loc_sem.at[2]),
        pltpu.make_async_copy(do_in.at[:, half(0)], dob.at[0, 0], loc_sem.at[3]),
    ]
    for copy in own:
        copy.start()
    xc = [(dx, dc) for dx in range(NX) for dc in range(2) if (dx, dc) != (0, 0)]
    partners = [dev(dx=dx, dc=dc) for dx, dc in xc]
    partners += [dev(dz=dz) for dz in range(1, NZ)] + [dev(dy=1), dev(dy=3)]
    barrier = pltpu.get_barrier_semaphore()
    for to in partners:
        pl.semaphore_signal(barrier, inc=1, device_id=to, device_id_type=MESH)
    pl.semaphore_wait(barrier, len(partners))
    for copy in own:
        copy.wait()

    mine = kvb.at[0, zrow(0)]
    for dz in Z_ORDER:
        send(mine, mine, z_ss.at[dz], z_rs.at[dz], dev(dz=dz))
    for dx, dc in sorted(xc, key=lambda m: (m[0] != 0, m[0] == 2)):
        slot = SLOT[(NX - dx) % NX]
        for i, (src, dst) in enumerate(((q_in, qb), (do_in, dob))):
            send(src.at[:, half(dc)], dst.at[slot, dc], q_ss.at[dx, dc, i], q_rs.at[slot, dc, i], dev(dx=dx, dc=dc))

    def spread(dz):
        block = kvb.at[0, zrow(dz)]
        send(block, kvb.at[0, zrow(dz, 1)], sb_ss.at[0, dz], sb_rs.at[0, dz], dev(dc=1))
        send(block, kvb.at[2, zrow(dz)], yk_ss.at[0, dz], yk_rs.at[0, dz], dev(dy=1))
        send(block, kvb.at[1, zrow(dz)], yk_ss.at[1, dz], yk_rs.at[1, dz], dev(dy=3))

    spread(0)
    for dz in Z_ORDER:
        arrive(kvb.at[0, zrow(dz)], z_rs.at[dz])
        spread(dz)

    def transposed(t):
        for i in range(2):
            rows, cols = pl.ds(i * 512, 512), pl.ds(t * KT + i * 512, 512)
            kt[:, cols] = kvb[t, rows, 0:DIM].T
            vt[0:DIM, cols] = kvb[t, rows, DIM : 2 * DIM].T

    def rows_of(ref, xo):
        return jnp.concatenate(
            [ref[xo, a, :, h * DIM : (h + 1) * DIM] for a in range(2) for h in range(4)], axis=0
        )

    def lanes(xo):
        return pl.ds(pl.multiple_of(xo * RB, RB), RB)

    def forward(xo, tiles, first=False):
        rows = lanes(xo)
        qs = rows_of(qb, xo)
        if not first:
            top, total = st[xo, 0:1, :], acc[:, rows]
        for t in tiles:
            s = nt(kvb[t, :, 0:DIM], qs)
            m = jnp.max(s, axis=0, keepdims=True) * LOG2_SCALE
            p = jnp.exp2(s * LOG2_SCALE - m).astype(BF16)
            w[pl.ds(t * KT, KT), rows] = p
            mt[t : t + 1, rows] = m
            a = nn(vt[:, t * KT : (t + 1) * KT], p)
            if first:
                top, total, first = m, a, False
            else:
                new = jnp.maximum(top, m)
                total = total * jnp.exp2(top - new) + a * jnp.exp2(m - new)
                top = new
        st[xo, 0:1, :] = top
        acc[:, rows] = total

    vt[DIM : DIM + 16, :] = jnp.ones((16, KEYS), BF16)
    mt[...] = jnp.zeros_like(mt)
    st[...] = jnp.zeros_like(st)
    for dz in (0,) + Z_ORDER:
        arrive(kvb.at[0, zrow(dz, 1)], sb_rs.at[0, dz])
    transposed(0)

    def arrive_rows(slot):
        for dc in range(2):
            if (slot, dc) != (0, 0):
                arrive(qb.at[slot, dc], q_rs.at[slot, dc, 0])
                arrive(dob.at[slot, dc], q_rs.at[slot, dc, 1])

    for slot in range(NX):
        arrive_rows(slot)

    def first_tile(xo, carry):
        forward(xo, (0,), True)
        return carry

    lax.fori_loop(0, 2, first_tile, 0)

    for n, dz in enumerate((0,) + Z_ORDER):
        for i, t in ((0, 2), (1, 1)):
            block = kvb.at[t, zrow(dz)]
            arrive(block, yk_rs.at[i, dz])
            send(block, kvb.at[t, zrow(dz, 1)], sb_ss.at[t, dz], sb_rs.at[t, dz], dev(dc=1))
            if n % 2 == i:
                send(block, kvb.at[3, zrow(dz)], y2_ss.at[dz], y2_rs.at[dz], dev(dy=1 if i == 0 else 3))

    lax.fori_loop(2, 4, first_tile, 0)

    for dz in (0,) + Z_ORDER:
        block = kvb.at[3, zrow(dz)]
        arrive(block, y2_rs.at[dz])
        send(block, kvb.at[3, zrow(dz, 1)], sb_ss.at[3, dz], sb_rs.at[3, dz], dev(dc=1))
    for t in (1, 2):
        for dz in (0,) + Z_ORDER:
            arrive(kvb.at[t, zrow(dz, 1)], sb_rs.at[t, dz])
        transposed(t)

    def middle_tiles(xo, carry):
        forward(xo, (1, 2))
        return carry

    lax.fori_loop(0, NX, middle_tiles, 0)
    for dz in (0,) + Z_ORDER:
        arrive(kvb.at[3, zrow(dz, 1)], sb_rs.at[3, dz])
    transposed(3)
    for xo in range(NX):
        forward(xo, (3,))
        rows = lanes(xo)
        st[xo, 1:2, :] = acc[DIM : DIM + 1, rows]
        grads = rows_of(dob, xo).astype(F32).T
        st[xo, 2:3, :] = jnp.sum(grads * acc[0:DIM, rows], axis=0, keepdims=True)
        for dx in (1, 3, 2):
            seen = SLOT[(NX - dx) % NX] - 1
            send(st.at[xo], sr.at[seen, xo], st_ss.at[dx - 1, xo], st_rs.at[seen, xo], dev(dx=dx))

    def totals(xo):
        rows = lanes(xo)
        parts = [st[xo]]
        for p in range(3):
            theirs = SLOT[(OFF[xo] - OFF[p + 1]) % NX]
            arrive(sr.at[p, theirs], st_rs.at[p, theirs])
            parts.append(sr[p, theirs])
        top = parts[0][0:1]
        for part in parts[1:]:
            top = jnp.maximum(top, part[0:1])
        total, dot = 0.0, 0.0
        for part in parts:
            factor = jnp.exp2(part[0:1] - top)
            total += part[1:2] * factor
            dot += part[2:3] * factor
        log_total = top + jnp.log2(total)
        lse[0:1, rows] = log_total
        rdn[0:1, rows] = dot / total
        f = jnp.exp2(mt[:, rows] - log_total)
        for i in range(RB // 128):
            part = jnp.concatenate([f[:, i * 128 : (i + 1) * 128], jnp.zeros((120, 128), F32)], axis=0)
            fcol[xo, i * 128 : (i + 1) * 128, :] = part.T

    def backward(xo, t, start):
        rows = lanes(xo)
        f = jnp.exp2(mt[t : t + 1, rows] - lse[0:1, rows])
        grads = (rows_of(dob, xo).astype(F32) * fcol[xo, :, t : t + 1]).astype(BF16)
        p = w[pl.ds(t * KT, KT), rows]
        pg = nt(kvb[t, :, DIM : 2 * DIM], grads) - f * rdn[0:1, rows]
        ds = p * pg.astype(BF16)
        dkv[t, :, DIM : 2 * DIM] += nn(p, grads)
        dkv[t, :, 0:DIM] += nn(ds, rows_of(qb, xo))
        d = nn(kt[:, t * KT : (t + 1) * KT], ds)
        if start:
            dqt[:, rows] = d
        else:
            dqt[:, rows] += d

    def loop(t, lo, hi):
        def step(xo, carry):
            backward(xo, t, False)
            return carry

        lax.fori_loop(lo, hi, step, 0, unroll=True)

    OWN = NZ * TOK
    factor = jnp.where(lax.broadcasted_iota(jnp.int32, (1, 2 * DIM), 1) < DIM, SCALE, 1.0)

    def to_sibling(t):
        sib_src[t] = (dkv[t, OWN:, :] * factor).astype(BF16)
        send(sib_src.at[t], sib.at[t], sib_ss.at[t], sib_rs.at[t], dev(dc=1))

    def chip_sum(t):
        arrive(sib.at[t], sib_rs.at[t])
        return dkv[t, 0:OWN, :] * factor + sib[t].astype(F32)

    H = OWN // 2
    for t in range(NY):
        dkv[t] = jnp.zeros((KT, 2 * DIM), F32)
    for xo in range(NX):
        totals(xo)
        backward(xo, 3, True)
    to_sibling(3)
    loop(1, 0, 2)
    r2_src[...] = chip_sum(3).astype(BF16)
    send(r2_src.at[0:H], r2.at[0], r2_ss.at[0], r2_rs.at[0], dev(dy=1))
    send(r2_src.at[H:], r2.at[1], r2_ss.at[1], r2_rs.at[1], dev(dy=3))
    loop(1, 2, 4)
    to_sibling(1)
    loop(2, 0, 2)
    part = chip_sum(1)
    arrive(r2.at[0], r2_rs.at[0])
    y_src[0, 0:H] = (part[0:H] + r2[0].astype(F32)).astype(BF16)
    y_src[0, H:] = part[H:].astype(BF16)
    send(y_src.at[0], yr.at[0], yr_ss.at[0], yr_rs.at[0], dev(dy=1))
    loop(2, 2, 4)
    to_sibling(2)

    def query_out(xo):
        d = (dqt[:, lanes(xo)] * SCALE).T
        for a in range(2):
            for h in range(4):
                n = a * 4 + h
                dq_src[xo, a, :, h * DIM : (h + 1) * DIM] = d[n * TOK : (n + 1) * TOK].astype(BF16)
        dx = OFF[xo]
        seen = SLOT[(NX - dx) % NX]
        for dc in range(2):
            if (dx, dc) != (0, 0):
                send(dq_src.at[xo, dc], dqr.at[seen, dc], dq_ss.at[xo, dc], dq_rs.at[seen, dc], dev(dx=dx, dc=dc))

    for n, xo in enumerate((3, 1, 2, 0)):
        backward(xo, 0, False)
        query_out(xo)
        if n == 1:
            part = chip_sum(2)
            arrive(r2.at[1], r2_rs.at[1])
            y_src[1, 0:H] = part[0:H].astype(BF16)
            y_src[1, H:] = (part[H:] + r2[1].astype(F32)).astype(BF16)
            send(y_src.at[1], yr.at[1], yr_ss.at[1], yr_rs.at[1], dev(dy=3))
    to_sibling(0)
    part = chip_sum(0)
    for i in range(2):
        arrive(yr.at[i], yr_rs.at[i])
        part += yr[i].astype(F32)
    z_src[...] = part.astype(BF16)
    dkv[0, 0:OWN, :] = part
    for dz in Z_ORDER:
        block = z_src.at[pl.ds(pl.multiple_of(lax.rem(z + dz, NZ) * TOK, TOK), TOK)]
        send(block, zr.at[dz - 1], zr_ss.at[dz], zr_rs.at[dz], dev(dz=dz))

    for dc in range(2):
        total = dq_src[0, 0].astype(F32) if dc == 0 else 0.0
        for slot in range(NX):
            if (slot, dc) != (0, 0):
                arrive(dqr.at[slot, dc], dq_rs.at[slot, dc])
                total += dqr[slot, dc].astype(F32)
        dq_out[:, half(dc)] = total.astype(BF16)
    total = dkv[0, pl.ds(pl.multiple_of(z * TOK, TOK), TOK), :]
    for dz in Z_ORDER:
        arrive(zr.at[dz - 1], zr_rs.at[dz])
        total += zr[dz - 1].astype(F32)
    dk_out[...] = total[:, 0:DIM].astype(BF16)
    dv_out[...] = total[:, DIM:].astype(BF16)
    for copy in pending:
        copy.wait_send()


def body(queries, key_vecs, value_vecs, out_grad):
    vmem, sem = pltpu.VMEM, pltpu.SemaphoreType.DMA
    out = lambda a: jax.ShapeDtypeStruct(a.shape, BF16)
    return pl.pallas_call(
        kernel,
        name="attention_backward",
        out_shape=[out(queries), out(key_vecs), out(value_vecs)],
        in_specs=[pl.BlockSpec(memory_space=vmem)] * 4,
        out_specs=[pl.BlockSpec(memory_space=vmem)] * 3,
        scratch_shapes=[
            vmem((NX, 2, TOK, HALF), BF16),
            vmem((NX, 2, TOK, HALF), BF16),
            vmem((NY, KT, 2 * DIM), BF16),
            vmem((DIM, KEYS), BF16),
            vmem((DIM + 16, KEYS), BF16),
            vmem((KEYS, ROWS), BF16),
            vmem((8, ROWS), F32),
            vmem((DIM + 16, ROWS), F32),
            vmem((NX, 8, RB), F32),
            vmem((NX - 1, NX, 8, RB), F32),
            vmem((8, ROWS), F32),
            vmem((8, ROWS), F32),
            vmem((NX, RB, 128), F32),
            vmem((DIM, ROWS), F32),
            vmem((NY, KT, 2 * DIM), F32),
            vmem((NY, KT // 2, 2 * DIM), BF16),
            vmem((NY, KT // 2, 2 * DIM), BF16),
            vmem((KT // 2, 2 * DIM), BF16),
            vmem((2, KT // 4, 2 * DIM), BF16),
            vmem((2, KT // 2, 2 * DIM), BF16),
            vmem((2, KT // 2, 2 * DIM), BF16),
            vmem((KT // 2, 2 * DIM), BF16),
            vmem((NZ - 1, TOK, 2 * DIM), BF16),
            vmem((NX, 2, TOK, HALF), BF16),
            vmem((NX, 2, TOK, HALF), BF16),
            sem((4,)),
            sem((NX, 2, 2)), sem((NX, 2, 2)),
            sem((NZ,)), sem((NZ,)),
            sem((NY, NZ)), sem((NY, NZ)),
            sem((2, NZ)), sem((2, NZ)),
            sem((NZ,)), sem((NZ,)),
            sem((NX - 1, NX)), sem((NX - 1, NX)),
            sem((NY,)), sem((NY,)),
            sem((2,)), sem((2,)),
            sem((2,)), sem((2,)),
            sem((NZ,)), sem((NZ,)),
            sem((NX, 2)), sem((NX, 2)),
        ],
        compiler_params=pltpu.CompilerParams(
            collective_id=0, has_side_effects=True, vmem_limit_bytes=60 * 2**20
        ),
    )(queries, out_grad, key_vecs, value_vecs)


def solution(mesh):
    spec = P(("ctx", "head"), None)
    return jax.shard_map(
        body, mesh=mesh, in_specs=(spec,) * 4, out_specs=(spec,) * 3, check_vma=False
    )
```

```python
import math

import jax
import jax.numpy as jnp
from jax import lax
from jax.experimental import pallas as pl
from jax.experimental.pallas import tpu as pltpu
from jax.sharding import PartitionSpec as P

F32, BF16 = jnp.float32, jnp.bfloat16
MESH = pl.DeviceIdType.MESH
NX, NY, NZ = 4, 4, 8
TOK = 64
DIM = 128
HALF = 512
RB = 512
KT = 1024
ROWS, KEYS = NX * RB, NY * KT
OFF = (0, 1, 3, 2)
SLOT = (0, 1, 3, 2)
SCALE = DIM**-0.5
LOG2_SCALE = SCALE * math.log2(math.e)
Z_ORDER = (1, 7, 2, 6, 3, 5, 4)
NEAR, FAR = (0, 1, 7, 2), (6, 3, 5, 4)
PLACE = {dz: (h, i) for h, part in enumerate((NEAR, FAR)) for i, dz in enumerate(part)}
SUB = 512


def nt(a, b):
    return lax.dot_general(a, b, (((1,), (1,)), ((), ())), preferred_element_type=F32)


def nn(a, b):
    return jnp.dot(a, b, preferred_element_type=F32)


def kernel(
    q_in, do_in, k_in, v_in, dq_out, dk_out, dv_out,
    qb, dob, kvb, kt, vt, w, sc, mt, acc, st, st_src, sr, lse, rdn, fcol, dqt, dkv,
    sib_src, sib, r2_src, r2, y_src, yr, z_own, z_src, zr, dq_src, dqr,
    loc_sem, q_ss, q_rs, z_ss, z_rs, sb_ss, sb_rs, yk_ss, yk_rs, y2_ss, y2_rs,
    st_ss, st_rs, sib_ss, sib_rs, r2_ss, r2_rs, yr_ss, yr_rs, zr_ss, zr_rs, dq_ss, dq_rs,
):
    ctx, hd = lax.axis_index("ctx"), lax.axis_index("head")
    y, z = ctx // (2 * NZ), lax.rem(ctx // 2, NZ)
    x, c = (hd // 2) * 2 + lax.rem(ctx, 2), lax.rem(hd, 2)

    def dev(dx=0, dy=0, dz=0, dc=0):
        xx, yy = lax.rem(x + dx, NX), lax.rem(y + dy, NY)
        zz, cc = lax.rem(z + dz, NZ), lax.rem(c + dc, 2)
        return ((yy * NZ + zz) * 2 + lax.rem(xx, 2), (xx // 2) * 2 + cc)

    pending = []

    def send(src, dst, ss, rs, to):
        copy = pltpu.make_async_remote_copy(
            src_ref=src, dst_ref=dst, send_sem=ss, recv_sem=rs,
            device_id=to, device_id_type=MESH,
        )
        copy.start()
        pending.append(copy)

    def arrive(ref, rs):
        pltpu.make_async_remote_copy(
            src_ref=ref, dst_ref=ref, send_sem=rs, recv_sem=rs,
            device_id=dev(dc=1), device_id_type=MESH,
        ).wait_recv()

    def half(dc):
        return pl.ds(pl.multiple_of(lax.rem(c + dc, 2) * HALF, HALF), HALF)

    own = [
        pltpu.make_async_copy(k_in, kvb.at[0, 0, 0, 0, :, 0:DIM], loc_sem.at[0]),
        pltpu.make_async_copy(v_in, kvb.at[0, 0, 0, 0, :, DIM : 2 * DIM], loc_sem.at[1]),
        pltpu.make_async_copy(q_in.at[:, half(0)], qb.at[x, 0], loc_sem.at[2]),
        pltpu.make_async_copy(do_in.at[:, half(0)], dob.at[x, 0], loc_sem.at[3]),
    ]
    for copy in own:
        copy.start()
    xc = [(dx, dc) for dx in range(NX) for dc in range(2) if (dx, dc) != (0, 0)]
    partners = [dev(dx=dx, dc=dc) for dx, dc in xc]
    partners += [dev(dz=dz) for dz in range(1, NZ)] + [dev(dy=1), dev(dy=3)]
    barrier = pltpu.get_barrier_semaphore()
    for to in partners:
        pl.semaphore_signal(barrier, inc=1, device_id=to, device_id_type=MESH)
    for copy in own:
        copy.wait()
    pl.semaphore_wait(barrier, len(partners))

    def block(t, dz, core=0):
        h, i = PLACE[dz]
        return kvb.at[t, h, core, i]

    def xat(off):
        return lax.rem(x + off, NX)

    def spread(dz):
        src = block(0, dz)
        send(src, block(2, dz), yk_ss.at[0, dz], yk_rs.at[0, dz], dev(dy=1))
        send(src, block(1, dz), yk_ss.at[1, dz], yk_rs.at[1, dz], dev(dy=3))
        send(src, block(0, dz, 1), sb_ss.at[0, dz], sb_rs.at[0, dz], dev(dc=1))

    for dz in Z_ORDER:
        send(block(0, 0), block(0, dz), z_ss.at[dz], z_rs.at[dz], dev(dz=dz))
    spread(0)
    for dx, dc in ((0, 1), (1, 0), (3, 0), (1, 1), (3, 1), (2, 0), (2, 1)):
        slot = SLOT[(NX - dx) % NX]
        for i, (src, dst) in enumerate(((q_in, qb), (do_in, dob))):
            send(src.at[:, half(dc)], dst.at[x, dc], q_ss.at[dx, dc, i], q_rs.at[slot, dc, i], dev(dx=dx, dc=dc))

    vt[DIM : DIM + 16, :] = jnp.ones((16, KEYS), BF16)
    st[...] = jnp.zeros_like(st)
    for t in range(NY):
        dkv[t] = jnp.zeros((KT, 2 * DIM), F32)
    for dz in Z_ORDER:
        arrive(block(0, dz), z_rs.at[dz])
        spread(dz)

    def keys_of(t, h):
        return kvb[t, h, :, :, :, 0:DIM].reshape(SUB, DIM)

    def values_of(t, h):
        return kvb[t, h, :, :, :, DIM : 2 * DIM].reshape(SUB, DIM)

    def span(t, h):
        return pl.ds(t * KT + h * SUB, SUB)

    def rows_of(ref, xo):
        return jnp.concatenate(
            [ref[xo, a, :, i * DIM : (i + 1) * DIM] for a in range(2) for i in range(4)], axis=0
        )

    def lanes(xo):
        return pl.ds(xo * RB if isinstance(xo, int) else pl.multiple_of(xo * RB, RB), RB)

    def forward(blocks):
        before = None
        for n, now in enumerate(list(blocks) + [None]):
            new_top, total = None, None
            if now is not None:
                qs = rows_of(qb, now[0])
            for i in range(2):
                if now is not None:
                    s = nt(keys_of(*now[1][i]), qs)
                    sc[n % 2, i] = s
                    top = jnp.max(s, axis=0, keepdims=True)
                    new_top = top if new_top is None else jnp.maximum(new_top, top)
                if before is not None:
                    xo, subs, _ = before
                    cols = span(*subs[i])
                    p = jnp.exp2(sc[(n + 1) % 2, i] * LOG2_SCALE - m).astype(BF16)
                    w[cols, lanes(xo)] = p
                    mt[2 * subs[i][0] + subs[i][1], lanes(xo)] = m[0]
                    a = nn(vt[:, cols], p)
                    total = a if total is None else total + a
            if before is not None:
                xo, _, first = before
                if first:
                    st[xo, 0:1, :] = m
                    acc[:, lanes(xo)] = total
                else:
                    old = st[xo, 0:1, :]
                    top = jnp.maximum(old, m)
                    acc[:, lanes(xo)] = acc[:, lanes(xo)] * jnp.exp2(old - top) + total * jnp.exp2(m - top)
                    st[xo, 0:1, :] = top
            if now is not None:
                m = new_top * LOG2_SCALE
            before = now

    def arrive_rows(slot):
        for dc in range(2):
            if (slot, dc) != (0, 0):
                arrive(qb.at[xat(OFF[slot]), dc], q_rs.at[slot, dc, 0])
                arrive(dob.at[xat(OFF[slot]), dc], q_rs.at[slot, dc, 1])

    def arrive_sibling(t, h):
        for dz in (NEAR, FAR)[h]:
            arrive(block(t, dz, 1), sb_rs.at[t, dz])
        kt[:, span(t, h)] = keys_of(t, h).T
        vt[0:DIM, span(t, h)] = values_of(t, h).T

    def from_y(part):
        for n, dz in enumerate(part):
            for i, t in ((0, 2), (1, 1)):
                src = block(t, dz)
                arrive(src, yk_rs.at[i, dz])
                if n % 2 == i:
                    send(src, block(3, dz), y2_ss.at[dz], y2_rs.at[dz], dev(dy=1 if i == 0 else 3))
                send(src, block(t, dz, 1), sb_ss.at[t, dz], sb_rs.at[t, dz], dev(dc=1))

    def from_far_y(part):
        for dz in part:
            src = block(3, dz)
            arrive(src, y2_rs.at[dz])
            send(src, block(3, dz, 1), sb_ss.at[3, dz], sb_rs.at[3, dz], dev(dc=1))

    G0, G1, G2, G3 = ((0, 0), (0, 1)), ((1, 0), (2, 0)), ((1, 1), (2, 1)), ((3, 0), (3, 1))
    from_y(NEAR)
    arrive_rows(0)
    arrive_sibling(0, 0)
    arrive_sibling(0, 1)
    arrive_rows(1)
    arrive_rows(2)
    forward([(xat(off), G0, True) for off in (0, 1, 3)])
    from_y(FAR)
    for t in (1, 2):
        arrive_sibling(t, 0)
    forward([(xat(off), G1, False) for off in (0, 1)])
    from_far_y(NEAR)
    arrive_rows(3)
    forward([(xat(3), G1, False), (xat(2), G0, True), (xat(2), G1, False)])
    from_far_y(FAR)
    for t in (1, 2):
        arrive_sibling(t, 1)
    forward([(xo, G2, False) for xo in range(NX)])
    for h in range(2):
        arrive_sibling(3, h)
    forward([(xo, G3, False) for xo in range(NX)])
    for xo in range(NX):
        rows = lanes(xo)
        grads = rows_of(dob, xo).astype(F32).T
        dot = jnp.sum(grads * acc[0:DIM, rows], axis=0, keepdims=True)
        for i, row in enumerate((st[xo, 0:1, :], acc[DIM : DIM + 1, rows], dot)):
            for j in range(4):
                st_src[xo, 4 * i + j : 4 * i + j + 1, :] = row[:, j * DIM : (j + 1) * DIM]
        for dx in (1, 3, 2):
            seen = SLOT[(NX - dx) % NX] - 1
            send(st_src.at[xo], sr.at[seen, xo], st_ss.at[dx - 1, xo], st_rs.at[seen, xo], dev(dx=dx))

    def totals(xo):
        rows = lanes(xo)
        parts = [st_src[xo]]
        for p in range(3):
            arrive(sr.at[p, xo], st_rs.at[p, xo])
            parts.append(sr[p, xo])
        top = parts[0][0:4]
        for part in parts[1:]:
            top = jnp.maximum(top, part[0:4])
        total, dot = 0.0, 0.0
        for part in parts:
            factor = jnp.exp2(part[0:4] - top)
            total += part[4:8] * factor
            dot += part[8:12] * factor
        wide = lambda a: jnp.concatenate([a[j : j + 1] for j in range(4)], axis=1)
        log_total = wide(top + jnp.log2(total))
        lse[0:1, rows] = log_total
        rdn[0:1, rows] = wide(dot / total)
        f = jnp.exp2(mt[:, rows] - log_total)
        for i in range(RB // 128):
            part = jnp.concatenate([f[:, i * 128 : (i + 1) * 128], jnp.zeros((120, 128), F32)], axis=0)
            fcol[xo, i * 128 : (i + 1) * 128, :] = part.T

    def backward(xo, t, h, start=False):
        rows = lanes(xo)
        sub = 2 * t + h
        f = jnp.exp2(mt[sub : sub + 1, rows] - lse[0:1, rows])
        grads = (rows_of(dob, xo).astype(F32) * fcol[xo, :, sub : sub + 1]).astype(BF16)
        p = w[span(t, h), rows]
        pg = nt(values_of(t, h), grads) - f * rdn[0:1, rows]
        ds = p * pg.astype(BF16)
        part = pl.ds(h * SUB, SUB)
        dkv[t, part, DIM : 2 * DIM] += nn(p, grads)
        dkv[t, part, 0:DIM] += nn(ds, rows_of(qb, xo))
        d = nn(kt[:, span(t, h)], ds)
        if start:
            dqt[:, rows] = d
        else:
            dqt[:, rows] += d

    OWN = SUB // 2
    factor = jnp.where(lax.broadcasted_iota(jnp.int32, (1, 2 * DIM), 1) < DIM, SCALE, 1.0)

    def to_sibling(t, h):
        sib_src[t, h] = (dkv[t, h * SUB + OWN : (h + 1) * SUB, :] * factor).astype(BF16)
        send(sib_src.at[t, h], sib.at[t, h], sib_ss.at[t, h], sib_rs.at[t, h], dev(dc=1))

    def chip_sum(t, h):
        arrive(sib.at[t, h], sib_rs.at[t, h])
        return dkv[t, h * SUB : h * SUB + OWN, :] * factor + sib[t, h].astype(F32)

    def to_far_y(h):
        r2_src[h] = chip_sum(3, h).reshape(2, OWN // 2, 2 * DIM).astype(BF16)
        for i in range(2):
            send(r2_src.at[h, i], r2.at[h, i], r2_ss.at[h, i], r2_rs.at[h, i], dev(dy=1 if i == 0 else 3))

    def to_y(t, h):
        i = t - 1
        part = chip_sum(t, h)
        arrive(r2.at[h, i], r2_rs.at[h, i])
        more = r2[h, i].astype(F32)
        lo, hi = part[0 : OWN // 2], part[OWN // 2 :]
        lo, hi = (lo + more, hi) if i == 0 else (lo, hi + more)
        y_src[i, h, 0 : OWN // 2] = lo.astype(BF16)
        y_src[i, h, OWN // 2 :] = hi.astype(BF16)
        send(y_src.at[i, h], yr.at[i, h], yr_ss.at[i, h], yr_rs.at[i, h], dev(dy=1 if t == 1 else 3))

    def half_tile(t, h):
        for xo in range(NX):
            backward(xo, t, h)
        to_sibling(t, h)

    for xo in range(NX):
        totals(xo)
        backward(xo, 3, 1, True)
    to_sibling(3, 1)
    half_tile(3, 0)
    to_far_y(1)
    half_tile(1, 1)
    to_far_y(0)
    half_tile(2, 1)
    to_y(1, 1)
    half_tile(1, 0)
    to_y(2, 1)
    half_tile(2, 0)
    to_y(1, 0)
    half_tile(0, 1)
    to_y(2, 0)

    def query_out(slot):
        dx = OFF[slot]
        d = (dqt[:, lanes(xat(dx))] * SCALE).T
        for a in range(2):
            for i in range(4):
                n = a * 4 + i
                dq_src[slot, a, :, i * DIM : (i + 1) * DIM] = d[n * TOK : (n + 1) * TOK].astype(BF16)
        seen = SLOT[(NX - dx) % NX]
        for dc in range(2):
            if (dx, dc) != (0, 0):
                send(dq_src.at[slot, dc], dqr.at[seen, dc], dq_ss.at[slot, dc], dq_rs.at[seen, dc], dev(dx=dx, dc=dc))

    def to_z(h):
        part = chip_sum(0, h)
        for i in range(2):
            arrive(yr.at[i, h], yr_rs.at[i, h])
            part += yr[i, h].astype(F32)
        if h == 0:
            z_own[...] = part[0:TOK]
        z_src[h] = part.astype(BF16).reshape(4, TOK, 2 * DIM)
        for dz in reversed((NEAR[1:], FAR)[h]):
            send(z_src.at[h, PLACE[dz][1]], zr.at[dz - 1], zr_ss.at[dz], zr_rs.at[dz], dev(dz=NZ - dz))

    for n, slot in enumerate((3, 1, 2, 0)):
        backward(xat(OFF[slot]), 0, 0)
        query_out(slot)
        if n == 2:
            to_z(1)
    to_sibling(0, 0)
    to_z(0)

    for dc in range(2):
        total = dq_src[0, 0].astype(F32) if dc == 0 else 0.0
        for slot in range(NX):
            if (slot, dc) != (0, 0):
                arrive(dqr.at[slot, dc], dq_rs.at[slot, dc])
                total += dqr[slot, dc].astype(F32)
        dq_out[:, half(dc)] = total.astype(BF16)
    total = z_own[...]
    for dz in reversed(Z_ORDER):
        arrive(zr.at[dz - 1], zr_rs.at[dz])
        total += zr[dz - 1].astype(F32)
    dk_out[...] = total[:, 0:DIM].astype(BF16)
    dv_out[...] = total[:, DIM:].astype(BF16)
    for copy in pending:
        copy.wait_send()


def body(queries, key_vecs, value_vecs, out_grad):
    vmem, sem = pltpu.VMEM, pltpu.SemaphoreType.DMA
    out = lambda a: jax.ShapeDtypeStruct(a.shape, BF16)
    return pl.pallas_call(
        kernel,
        name="attention_backward",
        out_shape=[out(queries), out(key_vecs), out(value_vecs)],
        in_specs=[pl.BlockSpec(memory_space=pl.ANY)] * 4,
        out_specs=[pl.BlockSpec(memory_space=vmem)] * 3,
        scratch_shapes=[
            vmem((NX, 2, TOK, HALF), BF16),
            vmem((NX, 2, TOK, HALF), BF16),
            vmem((NY, 2, 2, NZ // 2, TOK, 2 * DIM), BF16),
            vmem((DIM, KEYS), BF16),
            vmem((DIM + 16, KEYS), BF16),
            vmem((KEYS, ROWS), BF16),
            vmem((2, 2, SUB, RB), F32),
            vmem((8, ROWS), F32),
            vmem((DIM + 16, ROWS), F32),
            vmem((NX, 8, RB), F32),
            vmem((NX, 16, 128), F32),
            vmem((NX - 1, NX, 16, 128), F32),
            vmem((8, ROWS), F32),
            vmem((8, ROWS), F32),
            vmem((NX, RB, 128), F32),
            vmem((DIM, ROWS), F32),
            vmem((NY, KT, 2 * DIM), F32),
            vmem((NY, 2, KT // 4, 2 * DIM), BF16),
            vmem((NY, 2, KT // 4, 2 * DIM), BF16),
            vmem((2, 2, KT // 8, 2 * DIM), BF16),
            vmem((2, 2, KT // 8, 2 * DIM), BF16),
            vmem((2, 2, KT // 4, 2 * DIM), BF16),
            vmem((2, 2, KT // 4, 2 * DIM), BF16),
            vmem((TOK, 2 * DIM), F32),
            vmem((2, NZ // 2, TOK, 2 * DIM), BF16),
            vmem((NZ - 1, TOK, 2 * DIM), BF16),
            vmem((NX, 2, TOK, HALF), BF16),
            vmem((NX, 2, TOK, HALF), BF16),
            sem((4,)),
            sem((NX, 2, 2)), sem((NX, 2, 2)),
            sem((NZ,)), sem((NZ,)),
            sem((NY, NZ)), sem((NY, NZ)),
            sem((2, NZ)), sem((2, NZ)),
            sem((NZ,)), sem((NZ,)),
            sem((NX - 1, NX)), sem((NX - 1, NX)),
            sem((NY, 2)), sem((NY, 2)),
            sem((2, 2)), sem((2, 2)),
            sem((2, 2)), sem((2, 2)),
            sem((NZ,)), sem((NZ,)),
            sem((NX, 2)), sem((NX, 2)),
        ],
        compiler_params=pltpu.CompilerParams(
            collective_id=0, has_side_effects=True, vmem_limit_bytes=60 * 2**20
        ),
    )(queries, out_grad, key_vecs, value_vecs)


def solution(mesh):
    spec = P(("ctx", "head"), None)
    return jax.shard_map(
        body, mesh=mesh, in_specs=(spec,) * 4, out_specs=(spec,) * 3, check_vma=False
    )
```

```python
import math

import jax
import jax.numpy as jnp
from jax import lax
from jax.experimental import pallas as pl
from jax.experimental.pallas import tpu as pltpu
from jax.sharding import PartitionSpec as P

F32, BF16 = jnp.float32, jnp.bfloat16
MESH = pl.DeviceIdType.MESH
NX, NY, NZ = 4, 4, 8
TOK = 64
DIM = 128
HALF = 512
RB = 512
KT = 1024
ROWS, KEYS = NX * RB, NY * KT
OFF = (0, 1, 3, 2)
SLOT = (0, 1, 3, 2)
SCALE = DIM**-0.5
LOG2_SCALE = SCALE * math.log2(math.e)
Z_ORDER = (1, 7, 2, 6, 3, 5, 4)
NEAR, FAR = (0, 1, 7, 2), (6, 3, 5, 4)
PLACE = {dz: (h, i) for h, part in enumerate((NEAR, FAR)) for i, dz in enumerate(part)}
SUB = 512


def nt(a, b):
    return lax.dot_general(a, b, (((1,), (1,)), ((), ())), preferred_element_type=F32)


def nn(a, b):
    return jnp.dot(a, b, preferred_element_type=F32)


def kernel(
    q_in, do_in, k_in, v_in, dq_out, dk_out, dv_out,
    qb, dob, kvb, kt, vt, w, sc, mt, acc, st, st_src, sr, lse, rdn, fcol, dqt, dkv,
    sib_src, sib, r2_src, r2, y_src, yr, z_own, z_src, zr, dq_src, dqr,
    loc_sem, q_ss, q_rs, z_ss, z_rs, sb_ss, sb_rs, yk_ss, yk_rs, y2_ss, y2_rs,
    st_ss, st_rs, sib_ss, sib_rs, r2_ss, r2_rs, yr_ss, yr_rs, zr_ss, zr_rs, dq_ss, dq_rs,
):
    ctx, hd = lax.axis_index("ctx"), lax.axis_index("head")
    y, z = ctx // (2 * NZ), lax.rem(ctx // 2, NZ)
    x, c = (hd // 2) * 2 + lax.rem(ctx, 2), lax.rem(hd, 2)

    def dev(dx=0, dy=0, dz=0, dc=0):
        xx, yy = lax.rem(x + dx, NX), lax.rem(y + dy, NY)
        zz, cc = lax.rem(z + dz, NZ), lax.rem(c + dc, 2)
        return ((yy * NZ + zz) * 2 + lax.rem(xx, 2), (xx // 2) * 2 + cc)

    pending = []

    def send(src, dst, ss, rs, to):
        copy = pltpu.make_async_remote_copy(
            src_ref=src, dst_ref=dst, send_sem=ss, recv_sem=rs,
            device_id=to, device_id_type=MESH,
        )
        copy.start()
        pending.append(copy)

    def arrive(ref, rs):
        pltpu.make_async_remote_copy(
            src_ref=ref, dst_ref=ref, send_sem=rs, recv_sem=rs,
            device_id=dev(dc=1), device_id_type=MESH,
        ).wait_recv()

    def half(dc):
        return pl.ds(pl.multiple_of(lax.rem(c + dc, 2) * HALF, HALF), HALF)

    own = [
        pltpu.make_async_copy(k_in, kvb.at[0, 0, 0, 0, :, 0:DIM], loc_sem.at[0]),
        pltpu.make_async_copy(v_in, kvb.at[0, 0, 0, 0, :, DIM : 2 * DIM], loc_sem.at[1]),
        pltpu.make_async_copy(q_in.at[:, half(0)], qb.at[x, 0], loc_sem.at[2]),
        pltpu.make_async_copy(do_in.at[:, half(0)], dob.at[x, 0], loc_sem.at[3]),
    ]
    for copy in own:
        copy.start()
    xc = [(dx, dc) for dx in range(NX) for dc in range(2) if (dx, dc) != (0, 0)]
    partners = [dev(dx=dx, dc=dc) for dx, dc in xc]
    partners += [dev(dz=dz) for dz in range(1, NZ)] + [dev(dy=1), dev(dy=3)]
    barrier = pltpu.get_barrier_semaphore()
    for to in partners:
        pl.semaphore_signal(barrier, inc=1, device_id=to, device_id_type=MESH)
    for copy in own:
        copy.wait()
    pl.semaphore_wait(barrier, len(partners))

    def block(t, dz, core=0):
        h, i = PLACE[dz]
        return kvb.at[t, h, core, i]

    def xat(off):
        return lax.rem(x + off, NX)

    def spread(dz):
        src = block(0, dz)
        send(src, block(2, dz), yk_ss.at[0, dz], yk_rs.at[0, dz], dev(dy=1))
        send(src, block(1, dz), yk_ss.at[1, dz], yk_rs.at[1, dz], dev(dy=3))
        send(src, block(0, dz, 1), sb_ss.at[0, dz], sb_rs.at[0, dz], dev(dc=1))

    for dz in Z_ORDER:
        send(block(0, 0), block(0, dz), z_ss.at[dz], z_rs.at[dz], dev(dz=dz))
    spread(0)
    for dx, dc in ((0, 1), (1, 0), (3, 0), (1, 1), (3, 1), (2, 0), (2, 1)):
        slot = SLOT[(NX - dx) % NX]
        for i, (src, dst) in enumerate(((q_in, qb), (do_in, dob))):
            send(src.at[:, half(dc)], dst.at[x, dc], q_ss.at[dx, dc, i], q_rs.at[slot, dc, i], dev(dx=dx, dc=dc))

    vt[DIM : DIM + 16, :] = jnp.ones((16, KEYS), BF16)
    st[...] = jnp.zeros_like(st)
    for t in range(NY):
        dkv[t] = jnp.zeros((KT, 2 * DIM), F32)
    for dz in Z_ORDER:
        arrive(block(0, dz), z_rs.at[dz])
        spread(dz)

    def keys_of(t, h):
        return kvb[t, h, :, :, :, 0:DIM].reshape(SUB, DIM)

    def values_of(t, h):
        return kvb[t, h, :, :, :, DIM : 2 * DIM].reshape(SUB, DIM)

    def span(t, h):
        return pl.ds(t * KT + h * SUB, SUB)

    def rows_of(ref, xo):
        return jnp.concatenate(
            [ref[xo, a, :, i * DIM : (i + 1) * DIM] for a in range(2) for i in range(4)], axis=0
        )

    def lanes(xo):
        return pl.ds(xo * RB if isinstance(xo, int) else pl.multiple_of(xo * RB, RB), RB)

    def forward(blocks, finished=None):
        before = None
        for n, now in enumerate(list(blocks) + [None]):
            new_top, total = None, None
            if now is not None:
                qs = rows_of(qb, now[0])
            for i in range(2):
                if now is not None:
                    s = nt(keys_of(*now[1][i]), qs)
                    sc[n % 2, i] = s
                    top = jnp.max(s, axis=0, keepdims=True)
                    new_top = top if new_top is None else jnp.maximum(new_top, top)
                if before is not None:
                    xo, subs, _ = before
                    cols = span(*subs[i])
                    p = jnp.exp2(sc[(n + 1) % 2, i] * LOG2_SCALE - m).astype(BF16)
                    w[cols, lanes(xo)] = p
                    mt[2 * subs[i][0] + subs[i][1], lanes(xo)] = m[0]
                    a = nn(vt[:, cols], p)
                    total = a if total is None else total + a
            if before is not None:
                xo, _, first = before
                if first:
                    st[xo, 0:1, :] = m
                    acc[:, lanes(xo)] = total
                else:
                    old = st[xo, 0:1, :]
                    top = jnp.maximum(old, m)
                    acc[:, lanes(xo)] = acc[:, lanes(xo)] * jnp.exp2(old - top) + total * jnp.exp2(m - top)
                    st[xo, 0:1, :] = top
                if finished is not None:
                    finished(xo)
            if now is not None:
                m = new_top * LOG2_SCALE
            before = now

    def arrive_rows(slot):
        for dc in range(2):
            if (slot, dc) != (0, 0):
                arrive(qb.at[xat(OFF[slot]), dc], q_rs.at[slot, dc, 0])
                arrive(dob.at[xat(OFF[slot]), dc], q_rs.at[slot, dc, 1])

    def arrive_sibling(t, h):
        for dz in (NEAR, FAR)[h]:
            arrive(block(t, dz, 1), sb_rs.at[t, dz])
        kt[:, span(t, h)] = keys_of(t, h).T
        vt[0:DIM, span(t, h)] = values_of(t, h).T

    def from_y(part):
        for n, dz in enumerate(part):
            for i, t in ((0, 2), (1, 1)):
                src = block(t, dz)
                arrive(src, yk_rs.at[i, dz])
                if n % 2 == i:
                    send(src, block(3, dz), y2_ss.at[dz], y2_rs.at[dz], dev(dy=1 if i == 0 else 3))
                send(src, block(t, dz, 1), sb_ss.at[t, dz], sb_rs.at[t, dz], dev(dc=1))

    def from_far_y(part):
        for dz in part:
            src = block(3, dz)
            arrive(src, y2_rs.at[dz])
            send(src, block(3, dz, 1), sb_ss.at[3, dz], sb_rs.at[3, dz], dev(dc=1))

    G0, G1, G2, G3 = ((0, 0), (0, 1)), ((1, 0), (2, 0)), ((1, 1), (2, 1)), ((3, 0), (3, 1))
    from_y(NEAR)
    arrive_rows(0)
    arrive_sibling(0, 0)
    arrive_sibling(0, 1)
    arrive_rows(1)
    arrive_rows(2)
    forward([(xat(off), G0, True) for off in (0, 1, 3)])
    from_y(FAR)
    for t in (1, 2):
        arrive_sibling(t, 0)
    forward([(xat(off), G1, False) for off in (0, 1)])
    from_far_y(NEAR)
    arrive_rows(3)
    forward([(xat(3), G1, False), (xat(2), G0, True), (xat(2), G1, False)])
    from_far_y(FAR)
    for t in (1, 2):
        arrive_sibling(t, 1)
    forward([(xo, G2, False) for xo in range(NX)])
    for h in range(2):
        arrive_sibling(3, h)

    def exchange(xo):
        rows = lanes(xo)
        grads = rows_of(dob, xo).astype(F32).T
        dot = jnp.sum(grads * acc[0:DIM, rows], axis=0, keepdims=True)
        for i, row in enumerate((st[xo, 0:1, :], acc[DIM : DIM + 1, rows], dot)):
            for j in range(4):
                st_src[xo, 4 * i + j : 4 * i + j + 1, :] = row[:, j * DIM : (j + 1) * DIM]
        for dx in (1, 3, 2):
            seen = SLOT[(NX - dx) % NX] - 1
            send(st_src.at[xo], sr.at[seen, xo], st_ss.at[dx - 1, xo], st_rs.at[seen, xo], dev(dx=dx))

    forward([(xo, G3, False) for xo in range(NX)], exchange)

    def totals(xo):
        rows = lanes(xo)
        parts = [st_src[xo]]
        for p in range(3):
            arrive(sr.at[p, xo], st_rs.at[p, xo])
            parts.append(sr[p, xo])
        top = parts[0][0:4]
        for part in parts[1:]:
            top = jnp.maximum(top, part[0:4])
        total, dot = 0.0, 0.0
        for part in parts:
            factor = jnp.exp2(part[0:4] - top)
            total += part[4:8] * factor
            dot += part[8:12] * factor
        wide = lambda a: jnp.concatenate([a[j : j + 1] for j in range(4)], axis=1)
        log_total = wide(top + jnp.log2(total))
        lse[0:1, rows] = log_total
        rdn[0:1, rows] = wide(dot / total)
        f = jnp.exp2(mt[:, rows] - log_total)
        for i in range(RB // 128):
            part = jnp.concatenate([f[:, i * 128 : (i + 1) * 128], jnp.zeros((120, 128), F32)], axis=0)
            fcol[xo, i * 128 : (i + 1) * 128, :] = part.T

    def backward(xo, t, h, start=False):
        rows = lanes(xo)
        sub = 2 * t + h
        f = jnp.exp2(mt[sub : sub + 1, rows] - lse[0:1, rows])
        grads = (rows_of(dob, xo).astype(F32) * fcol[xo, :, sub : sub + 1]).astype(BF16)
        p = w[span(t, h), rows]
        pg = nt(values_of(t, h), grads) - f * rdn[0:1, rows]
        ds = p * pg.astype(BF16)
        part = pl.ds(h * SUB, SUB)
        dkv[t, part, DIM : 2 * DIM] += nn(p, grads)
        dkv[t, part, 0:DIM] += nn(ds, rows_of(qb, xo))
        d = nn(kt[:, span(t, h)], ds)
        if start:
            dqt[:, rows] = d
        else:
            dqt[:, rows] += d

    OWN = SUB // 2
    factor = jnp.where(lax.broadcasted_iota(jnp.int32, (1, 2 * DIM), 1) < DIM, SCALE, 1.0)

    def to_sibling(t, h):
        sib_src[t, h] = (dkv[t, h * SUB + OWN : (h + 1) * SUB, :] * factor).astype(BF16)
        send(sib_src.at[t, h], sib.at[t, h], sib_ss.at[t, h], sib_rs.at[t, h], dev(dc=1))

    def chip_sum(t, h):
        arrive(sib.at[t, h], sib_rs.at[t, h])
        return dkv[t, h * SUB : h * SUB + OWN, :] * factor + sib[t, h].astype(F32)

    def to_far_y(h):
        r2_src[h] = chip_sum(3, h).reshape(2, OWN // 2, 2 * DIM).astype(BF16)
        for i in range(2):
            send(r2_src.at[h, i], r2.at[h, i], r2_ss.at[h, i], r2_rs.at[h, i], dev(dy=1 if i == 0 else 3))

    def to_y(t, h):
        i = t - 1
        part = chip_sum(t, h)
        arrive(r2.at[h, i], r2_rs.at[h, i])
        more = r2[h, i].astype(F32)
        lo, hi = part[0 : OWN // 2], part[OWN // 2 :]
        lo, hi = (lo + more, hi) if i == 0 else (lo, hi + more)
        y_src[i, h, 0 : OWN // 2] = lo.astype(BF16)
        y_src[i, h, OWN // 2 :] = hi.astype(BF16)
        send(y_src.at[i, h], yr.at[i, h], yr_ss.at[i, h], yr_rs.at[i, h], dev(dy=1 if t == 1 else 3))

    def half_tile(t, h):
        for xo in range(NX):
            backward(xo, t, h)
        to_sibling(t, h)

    for xo in range(NX):
        totals(xo)
        backward(xo, 3, 1, True)
    to_sibling(3, 1)
    half_tile(3, 0)
    to_far_y(1)
    half_tile(1, 1)
    to_far_y(0)
    half_tile(2, 1)
    to_y(1, 1)
    half_tile(1, 0)
    to_y(2, 1)
    half_tile(2, 0)
    to_y(1, 0)
    half_tile(0, 1)
    to_y(2, 0)

    def query_out(slot):
        dx = OFF[slot]
        d = (dqt[:, lanes(xat(dx))] * SCALE).astype(BF16).T
        for a in range(2):
            for i in range(4):
                n = a * 4 + i
                dq_src[slot, a, :, i * DIM : (i + 1) * DIM] = d[n * TOK : (n + 1) * TOK]
        seen = SLOT[(NX - dx) % NX]
        for dc in range(2):
            if (dx, dc) != (0, 0):
                send(dq_src.at[slot, dc], dqr.at[seen, dc], dq_ss.at[slot, dc], dq_rs.at[seen, dc], dev(dx=dx, dc=dc))

    def to_z(h):
        part = chip_sum(0, h)
        for i in range(2):
            arrive(yr.at[i, h], yr_rs.at[i, h])
            part += yr[i, h].astype(F32)
        if h == 0:
            z_own[...] = part[0:TOK]
        z_src[h] = part.astype(BF16).reshape(4, TOK, 2 * DIM)
        for dz in reversed((NEAR[1:], FAR)[h]):
            send(z_src.at[h, PLACE[dz][1]], zr.at[dz - 1], zr_ss.at[dz], zr_rs.at[dz], dev(dz=NZ - dz))

    for slot in (3, 1, 2):
        backward(xat(OFF[slot]), 0, 0)
        query_out(slot)
    backward(xat(0), 0, 0)
    to_sibling(0, 0)
    to_z(1)
    query_out(0)
    to_z(0)

    for dc in range(2):
        total = dq_src[0, 0].astype(F32) if dc == 0 else 0.0
        for slot in range(NX):
            if (slot, dc) != (0, 0):
                arrive(dqr.at[slot, dc], dq_rs.at[slot, dc])
                total += dqr[slot, dc].astype(F32)
        dq_out[:, half(dc)] = total.astype(BF16)
    total = z_own[...]
    for dz in reversed(Z_ORDER):
        arrive(zr.at[dz - 1], zr_rs.at[dz])
        total += zr[dz - 1].astype(F32)
    dk_out[...] = total[:, 0:DIM].astype(BF16)
    dv_out[...] = total[:, DIM:].astype(BF16)
    for copy in pending:
        copy.wait_send()


def body(queries, key_vecs, value_vecs, out_grad):
    vmem, sem = pltpu.VMEM, pltpu.SemaphoreType.DMA
    out = lambda a: vmem(a.shape, BF16)
    return pl.pallas_call(
        kernel,
        name="attention_backward",
        out_shape=[out(queries), out(key_vecs), out(value_vecs)],
        in_specs=[pl.BlockSpec(memory_space=pl.ANY)] * 4,
        out_specs=[pl.BlockSpec(memory_space=vmem)] * 3,
        scratch_shapes=[
            vmem((NX, 2, TOK, HALF), BF16),
            vmem((NX, 2, TOK, HALF), BF16),
            vmem((NY, 2, 2, NZ // 2, TOK, 2 * DIM), BF16),
            vmem((DIM, KEYS), BF16),
            vmem((DIM + 16, KEYS), BF16),
            vmem((KEYS, ROWS), BF16),
            vmem((2, 2, SUB, RB), F32),
            vmem((8, ROWS), F32),
            vmem((DIM + 16, ROWS), F32),
            vmem((NX, 8, RB), F32),
            vmem((NX, 16, 128), F32),
            vmem((NX - 1, NX, 16, 128), F32),
            vmem((8, ROWS), F32),
            vmem((8, ROWS), F32),
            vmem((NX, RB, 128), F32),
            vmem((DIM, ROWS), F32),
            vmem((NY, KT, 2 * DIM), F32),
            vmem((NY, 2, KT // 4, 2 * DIM), BF16),
            vmem((NY, 2, KT // 4, 2 * DIM), BF16),
            vmem((2, 2, KT // 8, 2 * DIM), BF16),
            vmem((2, 2, KT // 8, 2 * DIM), BF16),
            vmem((2, 2, KT // 4, 2 * DIM), BF16),
            vmem((2, 2, KT // 4, 2 * DIM), BF16),
            vmem((TOK, 2 * DIM), F32),
            vmem((2, NZ // 2, TOK, 2 * DIM), BF16),
            vmem((NZ - 1, TOK, 2 * DIM), BF16),
            vmem((NX, 2, TOK, HALF), BF16),
            vmem((NX, 2, TOK, HALF), BF16),
            sem((4,)),
            sem((NX, 2, 2)), sem((NX, 2, 2)),
            sem((NZ,)), sem((NZ,)),
            sem((NY, NZ)), sem((NY, NZ)),
            sem((2, NZ)), sem((2, NZ)),
            sem((NZ,)), sem((NZ,)),
            sem((NX - 1, NX)), sem((NX - 1, NX)),
            sem((NY, 2)), sem((NY, 2)),
            sem((2, 2)), sem((2, 2)),
            sem((2, 2)), sem((2, 2)),
            sem((NZ,)), sem((NZ,)),
            sem((NX, 2)), sem((NX, 2)),
        ],
        compiler_params=pltpu.CompilerParams(
            collective_id=0, has_side_effects=True, vmem_limit_bytes=60 * 2**20
        ),
    )(queries, out_grad, key_vecs, value_vecs)


def solution(mesh):
    spec = P(("ctx", "head"), None)
    return jax.shard_map(
        body, mesh=mesh, in_specs=(spec,) * 4, out_specs=(spec,) * 3, check_vma=False
    )
```

```python
import math

import jax
import jax.numpy as jnp
from jax import lax
from jax.experimental import pallas as pl
from jax.experimental.pallas import tpu as pltpu
from jax.sharding import PartitionSpec as P

F32, BF16 = jnp.float32, jnp.bfloat16
MESH = pl.DeviceIdType.MESH
NX, NY, NZ = 4, 4, 8
TOK = 64
DIM = 128
HALF = 512
RB = 512
KT = 1024
ROWS, KEYS = NX * RB, NY * KT
OFF = (0, 1, 3, 2)
SLOT = (0, 1, 3, 2)
SCALE = DIM**-0.5
LOG2_SCALE = SCALE * math.log2(math.e)
Z_ORDER = (1, 7, 2, 6, 3, 5, 4)
NEAR, FAR = (0, 1, 7, 2), (6, 3, 5, 4)
PLACE = {dz: (h, i) for h, part in enumerate((NEAR, FAR)) for i, dz in enumerate(part)}
SUB = 512


def nt(a, b):
    return lax.dot_general(a, b, (((1,), (1,)), ((), ())), preferred_element_type=F32)


def nn(a, b):
    return jnp.dot(a, b, preferred_element_type=F32)


def kernel(
    q_in, do_in, k_in, v_in, dq_out, dkv_out,
    qb, dob, kvb, kt, vt, w, sc, dot_t, scaled, mt, acc, st, st_src, sr, lse, rdn, fcol, dqt, dkv,
    sib_src, sib, r2_src, r2, y_src, yr, z_own, z_src, zr, dq_src, dqr,
    loc_sem, q_ss, q_rs, z_ss, z_rs, sb_ss, sb_rs, yk_ss, yk_rs, y2_ss, y2_rs,
    st_ss, st_rs, sib_ss, sib_rs, r2_ss, r2_rs, yr_ss, yr_rs, zr_ss, zr_rs, dq_ss, dq_rs,
):
    ctx, hd = lax.axis_index("ctx"), lax.axis_index("head")
    y, z = ctx // (2 * NZ), lax.rem(ctx // 2, NZ)
    x, c = (hd // 2) * 2 + lax.rem(ctx, 2), lax.rem(hd, 2)

    def dev(dx=0, dy=0, dz=0, dc=0):
        xx, yy = lax.rem(x + dx, NX), lax.rem(y + dy, NY)
        zz, cc = lax.rem(z + dz, NZ), lax.rem(c + dc, 2)
        return ((yy * NZ + zz) * 2 + lax.rem(xx, 2), (xx // 2) * 2 + cc)

    pending = []

    def send(src, dst, ss, rs, to):
        copy = pltpu.make_async_remote_copy(
            src_ref=src, dst_ref=dst, send_sem=ss, recv_sem=rs,
            device_id=to, device_id_type=MESH,
        )
        copy.start()
        pending.append(copy)

    def arrive(ref, rs):
        pltpu.make_async_remote_copy(
            src_ref=ref, dst_ref=ref, send_sem=rs, recv_sem=rs,
            device_id=dev(dc=1), device_id_type=MESH,
        ).wait_recv()

    def half(dc):
        return pl.ds(pl.multiple_of(lax.rem(c + dc, 2) * HALF, HALF), HALF)

    own = [
        pltpu.make_async_copy(k_in, kvb.at[0, 0, 0, 0, :, 0:DIM], loc_sem.at[0]),
        pltpu.make_async_copy(v_in, kvb.at[0, 0, 0, 0, :, DIM : 2 * DIM], loc_sem.at[1]),
        pltpu.make_async_copy(q_in.at[:, half(0)], qb.at[x, 0], loc_sem.at[2]),
        pltpu.make_async_copy(do_in.at[:, half(0)], dob.at[x, 0], loc_sem.at[3]),
    ]
    for copy in own:
        copy.start()
    xc = [(dx, dc) for dx in range(NX) for dc in range(2) if (dx, dc) != (0, 0)]
    partners = [dev(dx=dx, dc=dc) for dx, dc in xc]
    partners += [dev(dz=dz) for dz in range(1, NZ)] + [dev(dy=1), dev(dy=3)]
    barrier = pltpu.get_barrier_semaphore()
    for to in partners:
        pl.semaphore_signal(barrier, inc=1, device_id=to, device_id_type=MESH)
    for copy in own:
        copy.wait()
    pl.semaphore_wait(barrier, len(partners))

    def block(t, dz, core=0):
        h, i = PLACE[dz]
        return kvb.at[t, h, core, i]

    def xat(off):
        return lax.rem(x + off, NX)

    def spread(dz):
        src = block(0, dz)
        send(src, block(2, dz), yk_ss.at[0, dz], yk_rs.at[0, dz], dev(dy=1))
        send(src, block(1, dz), yk_ss.at[1, dz], yk_rs.at[1, dz], dev(dy=3))
        send(src, block(0, dz, 1), sb_ss.at[0, dz], sb_rs.at[0, dz], dev(dc=1))

    for dz in Z_ORDER:
        send(block(0, 0), block(0, dz), z_ss.at[dz], z_rs.at[dz], dev(dz=dz))
    spread(0)
    for dx, dc in ((0, 1), (1, 0), (3, 0), (1, 1), (3, 1), (2, 0), (2, 1)):
        slot = SLOT[(NX - dx) % NX]
        for i, (src, dst) in enumerate(((q_in, qb), (do_in, dob))):
            send(src.at[:, half(dc)], dst.at[x, dc], q_ss.at[dx, dc, i], q_rs.at[slot, dc, i], dev(dx=dx, dc=dc))

    def rows_of(ref, xo):
        return jnp.concatenate(
            [ref[xo, a, :, i * DIM : (i + 1) * DIM] for a in range(2) for i in range(4)], axis=0
        )

    def lanes(xo):
        return pl.ds(xo * RB if isinstance(xo, int) else pl.multiple_of(xo * RB, RB), RB)

    def arrive_rows(slot):
        xo = xat(OFF[slot])
        for dc in range(2):
            if (slot, dc) != (0, 0):
                arrive(qb.at[xo, dc], q_rs.at[slot, dc, 0])
                arrive(dob.at[xo, dc], q_rs.at[slot, dc, 1])
        dot_t[:, lanes(xo)] = rows_of(dob, xo).T

    vt[DIM : DIM + 16, :] = jnp.ones((16, KEYS), BF16)
    st[...] = jnp.zeros_like(st)
    for t in range(NY):
        dkv[t] = jnp.zeros((KT, 2 * DIM), F32)
    arrive_rows(0)
    for dz in Z_ORDER:
        arrive(block(0, dz), z_rs.at[dz])
        spread(dz)

    def keys_of(t, h):
        return kvb[t, h, :, :, :, 0:DIM].reshape(SUB, DIM)

    def values_of(t, h):
        return kvb[t, h, :, :, :, DIM : 2 * DIM].reshape(SUB, DIM)

    def span(t, h):
        return pl.ds(t * KT + h * SUB, SUB)

    def forward(blocks, finished=None):
        before = None
        for n, now in enumerate(list(blocks) + [None]):
            new_top, total = None, None
            if now is not None:
                qs = rows_of(qb, now[0])
            for i in range(2):
                if now is not None:
                    s = nt(keys_of(*now[1][i]), qs)
                    sc[n % 2, i] = s
                    top = jnp.max(s, axis=0, keepdims=True)
                    new_top = top if new_top is None else jnp.maximum(new_top, top)
                if before is not None:
                    xo, subs, _ = before
                    cols = span(*subs[i])
                    p = jnp.exp2(sc[(n + 1) % 2, i] * LOG2_SCALE - m).astype(BF16)
                    w[cols, lanes(xo)] = p
                    mt[2 * subs[i][0] + subs[i][1], lanes(xo)] = m[0]
                    a = nn(vt[:, cols], p)
                    total = a if total is None else total + a
            if before is not None:
                xo, _, first = before
                if first:
                    st[xo, 0:1, :] = m
                    acc[:, lanes(xo)] = total
                else:
                    old = st[xo, 0:1, :]
                    top = jnp.maximum(old, m)
                    acc[:, lanes(xo)] = acc[:, lanes(xo)] * jnp.exp2(old - top) + total * jnp.exp2(m - top)
                    st[xo, 0:1, :] = top
                if finished is not None:
                    finished(xo)
            if now is not None:
                m = new_top * LOG2_SCALE
            before = now

    def arrive_sibling(t, h):
        for dz in (NEAR, FAR)[h]:
            arrive(block(t, dz, 1), sb_rs.at[t, dz])
        kt[:, span(t, h)] = keys_of(t, h).T
        vt[0:DIM, span(t, h)] = values_of(t, h).T

    def from_y(part):
        for n, dz in enumerate(part):
            for i, t in ((0, 2), (1, 1)):
                src = block(t, dz)
                arrive(src, yk_rs.at[i, dz])
                if n % 2 == i:
                    send(src, block(3, dz), y2_ss.at[dz], y2_rs.at[dz], dev(dy=1 if i == 0 else 3))
                send(src, block(t, dz, 1), sb_ss.at[t, dz], sb_rs.at[t, dz], dev(dc=1))

    def from_far_y(part):
        for dz in part:
            src = block(3, dz)
            arrive(src, y2_rs.at[dz])
            send(src, block(3, dz, 1), sb_ss.at[3, dz], sb_rs.at[3, dz], dev(dc=1))

    G0, G1, G2, G3 = ((0, 0), (0, 1)), ((1, 0), (2, 0)), ((1, 1), (2, 1)), ((3, 0), (3, 1))
    from_y(NEAR)
    arrive_sibling(0, 0)
    arrive_rows(1)
    arrive_rows(2)
    arrive_sibling(0, 1)
    forward([(xat(off), G0, True) for off in (0, 1, 3)])
    from_y(FAR)
    for t in (1, 2):
        arrive_sibling(t, 0)
    forward([(xat(off), G1, False) for off in (0, 1)])
    from_far_y(NEAR)
    arrive_rows(3)
    forward([(xat(3), G1, False), (xat(2), G0, True), (xat(2), G1, False)])
    from_far_y(FAR)
    for t in (1, 2):
        arrive_sibling(t, 1)
    forward([(xo, G2, False) for xo in range(NX)])
    for h in range(2):
        arrive_sibling(3, h)

    def exchange(xo):
        rows = lanes(xo)
        dot = jnp.sum(dot_t[:, rows].astype(F32) * acc[0:DIM, rows], axis=0, keepdims=True)
        for i, row in enumerate((st[xo, 0:1, :], acc[DIM : DIM + 1, rows], dot)):
            for j in range(4):
                st_src[xo, 4 * i + j : 4 * i + j + 1, :] = row[:, j * DIM : (j + 1) * DIM]
        for dx in (1, 3, 2):
            seen = SLOT[(NX - dx) % NX] - 1
            send(st_src.at[xo], sr.at[seen, xo], st_ss.at[dx - 1, xo], st_rs.at[seen, xo], dev(dx=dx))

    forward([(xo, G3, False) for xo in range(NX)], exchange)

    def totals(xo):
        rows = lanes(xo)
        parts = [st_src[xo]]
        for p in range(3):
            arrive(sr.at[p, xo], st_rs.at[p, xo])
            parts.append(sr[p, xo])
        top = parts[0][0:4]
        for part in parts[1:]:
            top = jnp.maximum(top, part[0:4])
        total, dot = 0.0, 0.0
        for part in parts:
            factor = jnp.exp2(part[0:4] - top)
            total += part[4:8] * factor
            dot += part[8:12] * factor
        wide = lambda a: jnp.concatenate([a[j : j + 1] for j in range(4)], axis=1)
        log_total = wide(top + jnp.log2(total))
        lse[0:1, rows] = log_total
        rdn[0:1, rows] = wide(dot / total)
        f = jnp.exp2(mt[:, rows] - log_total)
        for i in range(RB // 128):
            part = jnp.concatenate([f[:, i * 128 : (i + 1) * 128], jnp.zeros((120, 128), F32)], axis=0)
            fcol[xo, i * 128 : (i + 1) * 128, :] = part.T

    def backward(xo, t, h, start=False):
        rows = lanes(xo)
        sub = 2 * t + h
        f = jnp.exp2(mt[sub : sub + 1, rows] - lse[0:1, rows])
        if (t, h) in ((3, 1), (1, 1), (1, 0), (0, 1)):
            grads = (rows_of(dob, xo).astype(F32) * fcol[xo, :, sub : sub + 1]).astype(BF16)
            scaled[rows, :] = grads
        else:
            grads = scaled[rows, :]
        p = w[span(t, h), rows]
        pg = nt(values_of(t, h), grads) - f * rdn[0:1, rows]
        ds = p * pg.astype(BF16)
        part = pl.ds(h * SUB, SUB)
        dkv[t, part, DIM : 2 * DIM] += nn(p, grads)
        dkv[t, part, 0:DIM] += nn(ds, rows_of(qb, xo))
        d = nn(kt[:, span(t, h)], ds)
        if start:
            dqt[:, rows] = d
        else:
            dqt[:, rows] += d

    OWN = SUB // 2
    factor = jnp.where(lax.broadcasted_iota(jnp.int32, (1, 2 * DIM), 1) < DIM, SCALE, 1.0)

    def to_sibling(t, h):
        sib_src[t, h] = (dkv[t, h * SUB + OWN : (h + 1) * SUB, :] * factor).astype(BF16)
        send(sib_src.at[t, h], sib.at[t, h], sib_ss.at[t, h], sib_rs.at[t, h], dev(dc=1))

    def chip_sum(t, h):
        arrive(sib.at[t, h], sib_rs.at[t, h])
        return dkv[t, h * SUB : h * SUB + OWN, :] * factor + sib[t, h].astype(F32)

    def to_far_y(h):
        r2_src[h] = chip_sum(3, h).reshape(2, OWN // 2, 2 * DIM).astype(BF16)
        for i in range(2):
            send(r2_src.at[h, i], r2.at[h, i], r2_ss.at[h, i], r2_rs.at[h, i], dev(dy=1 if i == 0 else 3))

    def to_y(t, h):
        i = t - 1
        part = chip_sum(t, h)
        arrive(r2.at[h, i], r2_rs.at[h, i])
        more = r2[h, i].astype(F32)
        lo, hi = part[0 : OWN // 2], part[OWN // 2 :]
        lo, hi = (lo + more, hi) if i == 0 else (lo, hi + more)
        y_src[i, h, 0 : OWN // 2] = lo.astype(BF16)
        y_src[i, h, OWN // 2 :] = hi.astype(BF16)
        send(y_src.at[i, h], yr.at[i, h], yr_ss.at[i, h], yr_rs.at[i, h], dev(dy=1 if t == 1 else 3))

    def half_tile(t, h):
        for xo in range(NX):
            backward(xo, t, h)
        to_sibling(t, h)

    for xo in range(NX):
        totals(xo)
        backward(xo, 3, 1, True)
    to_sibling(3, 1)
    half_tile(3, 0)
    to_far_y(1)
    half_tile(1, 1)
    to_far_y(0)
    half_tile(2, 1)
    to_y(1, 1)
    half_tile(1, 0)
    to_y(2, 1)
    half_tile(2, 0)
    to_y(1, 0)
    half_tile(0, 1)
    to_y(2, 0)

    def query_out(slot):
        dx = OFF[slot]
        d = (dqt[:, lanes(xat(dx))] * SCALE).astype(BF16).T
        for a in range(2):
            for i in range(4):
                n = a * 4 + i
                dq_src[slot, a, :, i * DIM : (i + 1) * DIM] = d[n * TOK : (n + 1) * TOK]
        seen = SLOT[(NX - dx) % NX]
        for dc in range(2):
            if (dx, dc) != (0, 0):
                send(dq_src.at[slot, dc], dqr.at[seen, dc], dq_ss.at[slot, dc], dq_rs.at[seen, dc], dev(dx=dx, dc=dc))

    def to_z(h):
        part = chip_sum(0, h)
        for i in range(2):
            arrive(yr.at[i, h], yr_rs.at[i, h])
            part += yr[i, h].astype(F32)
        if h == 0:
            z_own[...] = part[0:TOK]
        z_src[h] = part.astype(BF16).reshape(4, TOK, 2 * DIM)
        for dz in reversed((NEAR[1:], FAR)[h]):
            send(z_src.at[h, PLACE[dz][1]], zr.at[dz - 1], zr_ss.at[dz], zr_rs.at[dz], dev(dz=NZ - dz))

    for slot in (3, 1, 2):
        backward(xat(OFF[slot]), 0, 0)
        query_out(slot)
    backward(xat(0), 0, 0)
    to_sibling(0, 0)
    to_z(1)
    query_out(0)
    to_z(0)

    for dc in range(2):
        total = dq_src[0, 0].astype(F32) if dc == 0 else 0.0
        for slot in range(NX):
            if (slot, dc) != (0, 0):
                arrive(dqr.at[slot, dc], dq_rs.at[slot, dc])
                total += dqr[slot, dc].astype(F32)
        dq_out[:, half(dc)] = total.astype(BF16)
    total = z_own[...]
    for dz in reversed(Z_ORDER):
        arrive(zr.at[dz - 1], zr_rs.at[dz])
        total += zr[dz - 1].astype(F32)
    dkv_out[...] = total
    for copy in pending:
        copy.wait_send()


def body(queries, key_vecs, value_vecs, out_grad):
    vmem, sem = pltpu.VMEM, pltpu.SemaphoreType.DMA
    query_grad, both = pl.pallas_call(
        kernel,
        name="attention_backward",
        out_shape=[vmem(queries.shape, BF16), vmem((TOK, 2 * DIM), F32)],
        in_specs=[pl.BlockSpec(memory_space=pl.ANY)] * 4,
        out_specs=[pl.BlockSpec(memory_space=vmem)] * 2,
        scratch_shapes=[
            vmem((NX, 2, TOK, HALF), BF16),
            vmem((NX, 2, TOK, HALF), BF16),
            vmem((NY, 2, 2, NZ // 2, TOK, 2 * DIM), BF16),
            vmem((DIM, KEYS), BF16),
            vmem((DIM + 16, KEYS), BF16),
            vmem((KEYS, ROWS), BF16),
            vmem((2, 2, SUB, RB), F32),
            vmem((DIM, ROWS), BF16),
            vmem((ROWS, DIM), BF16),
            vmem((8, ROWS), F32),
            vmem((DIM + 16, ROWS), F32),
            vmem((NX, 8, RB), F32),
            vmem((NX, 16, 128), F32),
            vmem((NX - 1, NX, 16, 128), F32),
            vmem((8, ROWS), F32),
            vmem((8, ROWS), F32),
            vmem((NX, RB, 128), F32),
            vmem((DIM, ROWS), F32),
            vmem((NY, KT, 2 * DIM), F32),
            vmem((NY, 2, KT // 4, 2 * DIM), BF16),
            vmem((NY, 2, KT // 4, 2 * DIM), BF16),
            vmem((2, 2, KT // 8, 2 * DIM), BF16),
            vmem((2, 2, KT // 8, 2 * DIM), BF16),
            vmem((2, 2, KT // 4, 2 * DIM), BF16),
            vmem((2, 2, KT // 4, 2 * DIM), BF16),
            vmem((TOK, 2 * DIM), F32),
            vmem((2, NZ // 2, TOK, 2 * DIM), BF16),
            vmem((NZ - 1, TOK, 2 * DIM), BF16),
            vmem((NX, 2, TOK, HALF), BF16),
            vmem((NX, 2, TOK, HALF), BF16),
            sem((4,)),
            sem((NX, 2, 2)), sem((NX, 2, 2)),
            sem((NZ,)), sem((NZ,)),
            sem((NY, NZ)), sem((NY, NZ)),
            sem((2, NZ)), sem((2, NZ)),
            sem((NZ,)), sem((NZ,)),
            sem((NX - 1, NX)), sem((NX - 1, NX)),
            sem((NY, 2)), sem((NY, 2)),
            sem((2, 2)), sem((2, 2)),
            sem((2, 2)), sem((2, 2)),
            sem((NZ,)), sem((NZ,)),
            sem((NX, 2)), sem((NX, 2)),
        ],
        compiler_params=pltpu.CompilerParams(
            collective_id=0, has_side_effects=True, vmem_limit_bytes=60 * 2**20
        ),
    )(queries, out_grad, key_vecs, value_vecs)
    return query_grad, both[:, :DIM].astype(BF16), both[:, DIM:].astype(BF16)


def solution(mesh):
    spec = P(("ctx", "head"), None)
    return jax.shard_map(
        body, mesh=mesh, in_specs=(spec,) * 4, out_specs=(spec,) * 3, check_vma=False
    )
```

```python
import math

import jax
import jax.numpy as jnp
from jax import lax
from jax.experimental import pallas as pl
from jax.experimental.pallas import tpu as pltpu
from jax.sharding import PartitionSpec as P

F32, BF16 = jnp.float32, jnp.bfloat16
MESH = pl.DeviceIdType.MESH
NX, NY, NZ = 4, 4, 8
TOK = 64
DIM = 128
HALF = 512
RB = 512
KT = 1024
ROWS, KEYS = NX * RB, NY * KT
OFF = (0, 1, 3, 2)
SLOT = (0, 1, 3, 2)
SCALE = DIM**-0.5
LOG2_SCALE = SCALE * math.log2(math.e)
Z_ORDER = (1, 7, 2, 6, 3, 5, 4)
NEAR, FAR = (0, 1, 7, 2), (6, 3, 5, 4)
PLACE = {dz: (h, i) for h, part in enumerate((NEAR, FAR)) for i, dz in enumerate(part)}
SUB = 512


def nt(a, b):
    return lax.dot_general(a, b, (((1,), (1,)), ((), ())), preferred_element_type=F32)


def nn(a, b):
    return jnp.dot(a, b, preferred_element_type=F32)


def kernel(
    q_in, do_in, k_in, v_in, dq_out, dkv_out,
    qb, dob, kvb, kt, vt, w, sc, dot_t, scaled, mt, acc, st, st_src, sr, lse, rdn, fcol, dqt, dkv,
    sib_src, sib, r2_src, r2, y_src, yr, z_own, z_src, zr, dq_src, dqr,
    loc_sem, q_ss, q_rs, z_ss, z_rs, sb_ss, sb_rs, yk_ss, yk_rs, y2_ss, y2_rs,
    st_ss, st_rs, sib_ss, sib_rs, r2_ss, r2_rs, yr_ss, yr_rs, zr_ss, zr_rs, dq_ss, dq_rs,
):
    ctx, hd = lax.axis_index("ctx"), lax.axis_index("head")
    y, z = ctx // (2 * NZ), lax.rem(ctx // 2, NZ)
    x, c = (hd // 2) * 2 + lax.rem(ctx, 2), lax.rem(hd, 2)

    def dev(dx=0, dy=0, dz=0, dc=0):
        xx, yy = lax.rem(x + dx, NX), lax.rem(y + dy, NY)
        zz, cc = lax.rem(z + dz, NZ), lax.rem(c + dc, 2)
        return ((yy * NZ + zz) * 2 + lax.rem(xx, 2), (xx // 2) * 2 + cc)

    pending = []

    def send(src, dst, ss, rs, to):
        copy = pltpu.make_async_remote_copy(
            src_ref=src, dst_ref=dst, send_sem=ss, recv_sem=rs,
            device_id=to, device_id_type=MESH,
        )
        copy.start()
        pending.append(copy)

    def arrive(ref, rs):
        pltpu.make_async_remote_copy(
            src_ref=ref, dst_ref=ref, send_sem=rs, recv_sem=rs,
            device_id=dev(dc=1), device_id_type=MESH,
        ).wait_recv()

    def half(dc):
        return pl.ds(pl.multiple_of(lax.rem(c + dc, 2) * HALF, HALF), HALF)

    own = [
        pltpu.make_async_copy(k_in, kvb.at[0, 0, 0, 0, :, 0:DIM], loc_sem.at[0]),
        pltpu.make_async_copy(v_in, kvb.at[0, 0, 0, 0, :, DIM : 2 * DIM], loc_sem.at[1]),
        pltpu.make_async_copy(q_in.at[:, half(0)], qb.at[x, 0], loc_sem.at[2]),
        pltpu.make_async_copy(do_in.at[:, half(0)], dob.at[x, 0], loc_sem.at[3]),
    ]
    xc = [(dx, dc) for dx in range(NX) for dc in range(2) if (dx, dc) != (0, 0)]
    partners = [dev(dx=dx, dc=dc) for dx, dc in xc]
    partners = [dev(dz=dz) for dz in (4, 3, 5, 2, 6, 1, 7)] + partners[::-1] + [dev(dy=1), dev(dy=3)]
    barrier = pltpu.get_barrier_semaphore()
    for to in partners:
        pl.semaphore_signal(barrier, inc=1, device_id=to, device_id_type=MESH)
    for copy in own:
        copy.start()
    for copy in own:
        copy.wait()
    pl.semaphore_wait(barrier, len(partners))

    def block(t, dz, core=0):
        h, i = PLACE[dz]
        return kvb.at[t, h, core, i]

    def xat(off):
        return lax.rem(x + off, NX)

    def spread(dz):
        src = block(0, dz)
        send(src, block(2, dz), yk_ss.at[0, dz], yk_rs.at[0, dz], dev(dy=1))
        send(src, block(1, dz), yk_ss.at[1, dz], yk_rs.at[1, dz], dev(dy=3))
        send(src, block(0, dz, 1), sb_ss.at[0, dz], sb_rs.at[0, dz], dev(dc=1))

    for dz in Z_ORDER:
        send(block(0, 0), block(0, dz), z_ss.at[dz], z_rs.at[dz], dev(dz=dz))
    spread(0)
    for dx, dc in ((0, 1), (1, 0), (3, 0), (1, 1), (3, 1), (2, 0), (2, 1)):
        slot = SLOT[(NX - dx) % NX]
        for i, (src, dst) in enumerate(((q_in, qb), (do_in, dob))):
            send(src.at[:, half(dc)], dst.at[x, dc], q_ss.at[dx, dc, i], q_rs.at[slot, dc, i], dev(dx=dx, dc=dc))

    def rows_of(ref, xo):
        return jnp.concatenate(
            [ref[xo, a, :, i * DIM : (i + 1) * DIM] for a in range(2) for i in range(4)], axis=0
        )

    def lanes(xo):
        return pl.ds(xo * RB if isinstance(xo, int) else pl.multiple_of(xo * RB, RB), RB)

    def arrive_rows(slot):
        xo = xat(OFF[slot])
        for dc in range(2):
            if (slot, dc) != (0, 0):
                arrive(qb.at[xo, dc], q_rs.at[slot, dc, 0])
                arrive(dob.at[xo, dc], q_rs.at[slot, dc, 1])
        dot_t[:, lanes(xo)] = rows_of(dob, xo).T

    vt[DIM : DIM + 16, :] = jnp.ones((16, KEYS), BF16)
    st[...] = jnp.zeros_like(st)
    for t in range(NY):
        dkv[t] = jnp.zeros((KT, 2 * DIM), F32)
    arrive_rows(0)
    for dz in Z_ORDER:
        arrive(block(0, dz), z_rs.at[dz])
        spread(dz)

    def keys_of(t, h):
        return kvb[t, h, :, :, :, 0:DIM].reshape(SUB, DIM)

    def values_of(t, h):
        return kvb[t, h, :, :, :, DIM : 2 * DIM].reshape(SUB, DIM)

    def span(t, h):
        return pl.ds(t * KT + h * SUB, SUB)

    def forward(blocks, finished=None):
        before = None
        for n, now in enumerate(list(blocks) + [None]):
            new_top, total = None, None
            if now is not None:
                qs = rows_of(qb, now[0])
            for i in range(2):
                if now is not None:
                    s = nt(keys_of(*now[1][i]), qs)
                    sc[n % 2, i] = s
                    top = jnp.max(s, axis=0, keepdims=True)
                    new_top = top if new_top is None else jnp.maximum(new_top, top)
                if before is not None:
                    xo, subs, _ = before
                    cols = span(*subs[i])
                    p = jnp.exp2(sc[(n + 1) % 2, i] * LOG2_SCALE - m).astype(BF16)
                    w[cols, lanes(xo)] = p
                    mt[2 * subs[i][0] + subs[i][1], lanes(xo)] = m[0]
                    a = nn(vt[:, cols], p)
                    total = a if total is None else total + a
            if before is not None:
                xo, _, first = before
                if first:
                    st[xo, 0:1, :] = m
                    acc[:, lanes(xo)] = total
                else:
                    old = st[xo, 0:1, :]
                    top = jnp.maximum(old, m)
                    acc[:, lanes(xo)] = acc[:, lanes(xo)] * jnp.exp2(old - top) + total * jnp.exp2(m - top)
                    st[xo, 0:1, :] = top
                if finished is not None:
                    finished(xo)
            if now is not None:
                m = new_top * LOG2_SCALE
            before = now

    def arrive_sibling(t, h):
        for dz in (NEAR, FAR)[h]:
            arrive(block(t, dz, 1), sb_rs.at[t, dz])
        kt[:, span(t, h)] = keys_of(t, h).T
        vt[0:DIM, span(t, h)] = values_of(t, h).T

    def from_y(part):
        for n, dz in enumerate(part):
            for i, t in ((0, 2), (1, 1)):
                src = block(t, dz)
                arrive(src, yk_rs.at[i, dz])
                if n % 2 == i:
                    send(src, block(3, dz), y2_ss.at[dz], y2_rs.at[dz], dev(dy=1 if i == 0 else 3))
                send(src, block(t, dz, 1), sb_ss.at[t, dz], sb_rs.at[t, dz], dev(dc=1))

    def from_far_y(part):
        for dz in part:
            src = block(3, dz)
            arrive(src, y2_rs.at[dz])
            send(src, block(3, dz, 1), sb_ss.at[3, dz], sb_rs.at[3, dz], dev(dc=1))

    G0, G1, G2, G3 = ((0, 0), (0, 1)), ((1, 0), (2, 0)), ((1, 1), (2, 1)), ((3, 0), (3, 1))
    from_y(NEAR)
    arrive_sibling(0, 0)
    arrive_rows(1)
    arrive_rows(2)
    arrive_sibling(0, 1)
    forward([(xat(off), G0, True) for off in (0, 1, 3)])
    from_y(FAR)
    for t in (1, 2):
        arrive_sibling(t, 0)
    forward([(xat(off), G1, False) for off in (0, 1)])
    from_far_y(NEAR)
    arrive_rows(3)
    forward([(xat(3), G1, False), (xat(2), G0, True), (xat(2), G1, False)])
    from_far_y(FAR)
    for t in (1, 2):
        arrive_sibling(t, 1)
    forward([(xo, G2, False) for xo in range(NX)])
    for h in range(2):
        arrive_sibling(3, h)

    def exchange(xo):
        rows = lanes(xo)
        dot = jnp.sum(dot_t[:, rows].astype(F32) * acc[0:DIM, rows], axis=0, keepdims=True)
        for i, row in enumerate((st[xo, 0:1, :], acc[DIM : DIM + 1, rows], dot)):
            for j in range(4):
                st_src[xo, 4 * i + j : 4 * i + j + 1, :] = row[:, j * DIM : (j + 1) * DIM]
        for dx in (1, 3, 2):
            seen = SLOT[(NX - dx) % NX] - 1
            send(st_src.at[xo], sr.at[seen, xo], st_ss.at[dx - 1, xo], st_rs.at[seen, xo], dev(dx=dx))

    forward([(xo, G3, False) for xo in range(NX)], exchange)

    def totals(xo):
        rows = lanes(xo)
        parts = [st_src[xo]]
        for p in range(3):
            arrive(sr.at[p, xo], st_rs.at[p, xo])
            parts.append(sr[p, xo])
        top = parts[0][0:4]
        for part in parts[1:]:
            top = jnp.maximum(top, part[0:4])
        total, dot = 0.0, 0.0
        for part in parts:
            factor = jnp.exp2(part[0:4] - top)
            total += part[4:8] * factor
            dot += part[8:12] * factor
        wide = lambda a: jnp.concatenate([a[j : j + 1] for j in range(4)], axis=1)
        log_total = wide(top + jnp.log2(total))
        lse[0:1, rows] = log_total
        rdn[0:1, rows] = wide(dot / total)
        f = jnp.exp2(mt[:, rows] - log_total)
        for i in range(RB // 128):
            part = jnp.concatenate([f[:, i * 128 : (i + 1) * 128], jnp.zeros((120, 128), F32)], axis=0)
            fcol[xo, i * 128 : (i + 1) * 128, :] = part.T

    def backward(xo, t, h, start=False):
        rows = lanes(xo)
        sub = 2 * t + h
        f = jnp.exp2(mt[sub : sub + 1, rows] - lse[0:1, rows])
        if (t, h) in ((3, 1), (1, 1), (1, 0), (0, 1)):
            grads = (rows_of(dob, xo).astype(F32) * fcol[xo, :, sub : sub + 1]).astype(BF16)
            scaled[rows, :] = grads
        else:
            grads = scaled[rows, :]
        p = w[span(t, h), rows]
        pg = nt(values_of(t, h), grads) - f * rdn[0:1, rows]
        ds = p * pg.astype(BF16)
        part = pl.ds(h * SUB, SUB)
        dkv[t, part, DIM : 2 * DIM] += nn(p, grads)
        dkv[t, part, 0:DIM] += nn(ds, rows_of(qb, xo))
        d = nn(kt[:, span(t, h)], ds)
        if start:
            dqt[:, rows] = d
        else:
            dqt[:, rows] += d

    OWN = SUB // 2
    factor = jnp.where(lax.broadcasted_iota(jnp.int32, (1, 2 * DIM), 1) < DIM, SCALE, 1.0)

    def to_sibling(t, h):
        sib_src[t, h] = (dkv[t, h * SUB + OWN : (h + 1) * SUB, :] * factor).astype(BF16)
        send(sib_src.at[t, h], sib.at[t, h], sib_ss.at[t, h], sib_rs.at[t, h], dev(dc=1))

    def chip_sum(t, h):
        arrive(sib.at[t, h], sib_rs.at[t, h])
        return dkv[t, h * SUB : h * SUB + OWN, :] * factor + sib[t, h].astype(F32)

    def to_far_y(h):
        r2_src[h] = chip_sum(3, h).reshape(2, OWN // 2, 2 * DIM).astype(BF16)
        for i in range(2):
            send(r2_src.at[h, i], r2.at[h, i], r2_ss.at[h, i], r2_rs.at[h, i], dev(dy=1 if i == 0 else 3))

    def to_y(t, h):
        i = t - 1
        part = chip_sum(t, h)
        arrive(r2.at[h, i], r2_rs.at[h, i])
        more = r2[h, i].astype(F32)
        lo, hi = part[0 : OWN // 2], part[OWN // 2 :]
        lo, hi = (lo + more, hi) if i == 0 else (lo, hi + more)
        y_src[i, h, 0 : OWN // 2] = lo.astype(BF16)
        y_src[i, h, OWN // 2 :] = hi.astype(BF16)
        send(y_src.at[i, h], yr.at[i, h], yr_ss.at[i, h], yr_rs.at[i, h], dev(dy=1 if t == 1 else 3))

    def half_tile(t, h):
        for xo in range(NX):
            backward(xo, t, h)
        to_sibling(t, h)

    for xo in range(NX):
        totals(xo)
        backward(xo, 3, 1, True)
    to_sibling(3, 1)
    half_tile(3, 0)
    to_far_y(1)
    half_tile(1, 1)
    to_far_y(0)
    half_tile(2, 1)
    to_y(1, 1)
    half_tile(1, 0)
    to_y(2, 1)
    half_tile(2, 0)
    to_y(1, 0)
    half_tile(0, 1)
    to_y(2, 0)

    def query_out(slot):
        dx = OFF[slot]
        d = (dqt[:, lanes(xat(dx))] * SCALE).astype(BF16).T
        for a in range(2):
            for i in range(4):
                n = a * 4 + i
                dq_src[slot, a, :, i * DIM : (i + 1) * DIM] = d[n * TOK : (n + 1) * TOK]
        seen = SLOT[(NX - dx) % NX]
        for dc in range(2):
            if (dx, dc) != (0, 0):
                send(dq_src.at[slot, dc], dqr.at[seen, dc], dq_ss.at[slot, dc], dq_rs.at[seen, dc], dev(dx=dx, dc=dc))

    def to_z(h):
        part = chip_sum(0, h)
        for i in range(2):
            arrive(yr.at[i, h], yr_rs.at[i, h])
            part += yr[i, h].astype(F32)
        if h == 0:
            z_own[...] = part[0:TOK]
        z_src[h] = part.astype(BF16).reshape(4, TOK, 2 * DIM)
        for dz in reversed((NEAR[1:], FAR)[h]):
            send(z_src.at[h, PLACE[dz][1]], zr.at[dz - 1], zr_ss.at[dz], zr_rs.at[dz], dev(dz=NZ - dz))

    gone = len(pending)
    for slot in (3, 1, 2):
        backward(xat(OFF[slot]), 0, 0)
        query_out(slot)
    backward(xat(0), 0, 0)
    to_sibling(0, 0)
    to_z(1)
    query_out(0)
    to_z(0)
    for copy in pending[:gone]:
        copy.wait_send()

    for dc in range(2):
        total = dq_src[0, 0].astype(F32) if dc == 0 else 0.0
        for slot in range(NX):
            if (slot, dc) != (0, 0):
                arrive(dqr.at[slot, dc], dq_rs.at[slot, dc])
                total += dqr[slot, dc].astype(F32)
        dq_out[:, half(dc)] = total.astype(BF16)
    total = z_own[...]
    for dz in reversed(Z_ORDER):
        arrive(zr.at[dz - 1], zr_rs.at[dz])
        total += zr[dz - 1].astype(F32)
    dkv_out[...] = total
    for copy in pending[gone:]:
        copy.wait_send()


def body(queries, key_vecs, value_vecs, out_grad):
    vmem, sem = pltpu.VMEM, pltpu.SemaphoreType.DMA
    query_grad, both = pl.pallas_call(
        kernel,
        name="attention_backward",
        out_shape=[vmem(queries.shape, BF16), vmem((TOK, 2 * DIM), F32)],
        in_specs=[pl.BlockSpec(memory_space=pl.ANY)] * 4,
        out_specs=[pl.BlockSpec(memory_space=vmem)] * 2,
        scratch_shapes=[
            vmem((NX, 2, TOK, HALF), BF16),
            vmem((NX, 2, TOK, HALF), BF16),
            vmem((NY, 2, 2, NZ // 2, TOK, 2 * DIM), BF16),
            vmem((DIM, KEYS), BF16),
            vmem((DIM + 16, KEYS), BF16),
            vmem((KEYS, ROWS), BF16),
            vmem((2, 2, SUB, RB), F32),
            vmem((DIM, ROWS), BF16),
            vmem((ROWS, DIM), BF16),
            vmem((8, ROWS), F32),
            vmem((DIM + 16, ROWS), F32),
            vmem((NX, 8, RB), F32),
            vmem((NX, 16, 128), F32),
            vmem((NX - 1, NX, 16, 128), F32),
            vmem((8, ROWS), F32),
            vmem((8, ROWS), F32),
            vmem((NX, RB, 128), F32),
            vmem((DIM, ROWS), F32),
            vmem((NY, KT, 2 * DIM), F32),
            vmem((NY, 2, KT // 4, 2 * DIM), BF16),
            vmem((NY, 2, KT // 4, 2 * DIM), BF16),
            vmem((2, 2, KT // 8, 2 * DIM), BF16),
            vmem((2, 2, KT // 8, 2 * DIM), BF16),
            vmem((2, 2, KT // 4, 2 * DIM), BF16),
            vmem((2, 2, KT // 4, 2 * DIM), BF16),
            vmem((TOK, 2 * DIM), F32),
            vmem((2, NZ // 2, TOK, 2 * DIM), BF16),
            vmem((NZ - 1, TOK, 2 * DIM), BF16),
            vmem((NX, 2, TOK, HALF), BF16),
            vmem((NX, 2, TOK, HALF), BF16),
            sem((4,)),
            sem((NX, 2, 2)), sem((NX, 2, 2)),
            sem((NZ,)), sem((NZ,)),
            sem((NY, NZ)), sem((NY, NZ)),
            sem((2, NZ)), sem((2, NZ)),
            sem((NZ,)), sem((NZ,)),
            sem((NX - 1, NX)), sem((NX - 1, NX)),
            sem((NY, 2)), sem((NY, 2)),
            sem((2, 2)), sem((2, 2)),
            sem((2, 2)), sem((2, 2)),
            sem((NZ,)), sem((NZ,)),
            sem((NX, 2)), sem((NX, 2)),
        ],
        compiler_params=pltpu.CompilerParams(
            collective_id=0, has_side_effects=True, vmem_limit_bytes=60 * 2**20
        ),
    )(queries, out_grad, key_vecs, value_vecs)
    return query_grad, both[:, :DIM].astype(BF16), both[:, DIM:].astype(BF16)


def solution(mesh):
    spec = P(("ctx", "head"), None)
    return jax.shard_map(
        body, mesh=mesh, in_specs=(spec,) * 4, out_specs=(spec,) * 3, check_vma=False
    )
```
